32 devices in a mesh: frame: 8 (over y, x, core), head: 4 (over z).
Axes of the slice: x: 2, y: 2, z: 4, core: 2. Of those that a mesh axis runs over, the one named last changes fastest.
Arguments:
- queries: bfloat16 [16, 512, 3072], P('frame', None, 'head'), may hold values from -24 to 24
- keys: bfloat16 [16, 512, 3072], P('frame', None, 'head'), may hold values from -24 to 24
- values: bfloat16 [16, 512, 3072], P('frame', None, 'head'), may hold values from -6 to 6
- ref_keys: bfloat16 [512, 3072], P('frame', 'head'), may hold values from -24 to 24
- ref_values: bfloat16 [512, 3072], P('frame', 'head'), may hold values from -6 to 6
- rate_scale: float32 [24], P('head'), may hold values from 0.05 to 2
- rate_reach: float32 [24], P('head'), may hold values from 0.1 to 4
- window_start: int32 [16], replicated, may hold values from 0 to 15, as said below
- out_weight: bfloat16 [3072, 3072], P('head'), may hold values from -0.15625 to 0.15625
- conv_taps: float32 [3, 3072], P(None, 'head'), may hold values from -3 to 3
- cotangent: bfloat16 [16, 512, 3072], P('frame', None, 'head'), may hold values from -6 to 6
Outputs:
- block_out: bfloat16 [16, 512, 3072], P('frame', None, 'head')
- grad_queries: bfloat16 [16, 512, 3072], P('frame', None, 'head')
- grad_keys: bfloat16 [16, 512, 3072], P('frame', None, 'head')
- grad_values: bfloat16 [16, 512, 3072], P('frame', None, 'head')
- grad_ref_keys: float32 [512, 3072], P('frame', 'head')
- grad_ref_values: float32 [512, 3072], P('frame', 'head')
- grad_out_weight: float32 [3072, 3072], P('head', 'frame')
- grad_conv_taps: float32 [3, 3072], P(None, 'head')
The draws below stay inside these ranges and needn't reach their ends.
Inputs may be any that keep to these rules, and one draw needn't show every extreme that they name: window_start[f] <= f for every frame f.
All inputs are finite; a program needn't handle non-finite values.
Results may differ from the reference program's by a relative error of at most 0.015.
Values may be sent and summed in bfloat16 or wider, within the bound.
No kernel may reach another device: no remote copies, remote signals or barrier semaphores. Data moves between devices by JAX's collectives and lax.ppermute only.
A program may use at most 128 MiB of HBM per device.

```python
import math
import jax
import jax.numpy as jnp
from jax import lax

HEADS = 24
HEAD_DIM = 128
WIDTH = 3072
TAPS = 3
SPATIAL = 512
FRAMES = 16


def draw_queries(key, part):
    noise = jnp.clip(jax.random.normal(jax.random.fold_in(key, 11), (FRAMES, SPATIAL, WIDTH), jnp.float32), -4.0, 4.0)
    return noise.astype(jnp.bfloat16)


def draw_keys(key, part):
    noise = jnp.clip(jax.random.normal(jax.random.fold_in(key, 12), (FRAMES, SPATIAL, WIDTH), jnp.float32), -4.0, 4.0)
    return noise.astype(jnp.bfloat16)


def draw_ref_keys(key, part):
    noise = jnp.clip(jax.random.normal(jax.random.fold_in(key, 13), (SPATIAL, WIDTH), jnp.float32), -4.0, 4.0)
    return noise.astype(jnp.bfloat16)


def draw_window_start(key, part):
    backward_reach = jax.random.randint(jax.random.fold_in(key, 23), (FRAMES,), 0, FRAMES)
    places = jnp.arange(FRAMES, dtype=jnp.int32)
    backward_reach = jnp.where(places == FRAMES - 1, 0, backward_reach)
    return jnp.maximum(places - backward_reach, 0).astype(jnp.int32)


def raised(entries, own_key, source, target, parts, factor):
    def block_of(position):
        return (jnp.arange(entries.shape[position]) // (entries.shape[position] // parts)).reshape((-1,) + (1,) * (entries.ndim - 1 - position))

    first = jax.random.permutation(own_key, parts)[block_of(target)]
    far = (block_of(target) + parts // 2) % parts
    return jnp.where((block_of(source) == first) | (block_of(source) == far), factor * entries, entries)


def steps_of(stream_key, shape, cuts, low, largest):
    def one(position, parts):
        heights = jax.random.uniform(jax.random.fold_in(jax.random.fold_in(stream_key, 6), position), (parts,), jnp.float32, low / len(cuts), largest / len(cuts))
        return jnp.repeat(jnp.exp(heights), shape[position] // parts).reshape((-1,) + (1,) * (len(shape) - position - 1))

    gain = one(*cuts[0])
    for cut in cuts[1:]:
        gain = gain * one(*cut)
    return gain


def bell_draw(rng, extent, spread, most, cuts=(), kind=jnp.bfloat16):
    values = jax.random.normal(rng, extent, jnp.float32) * spread
    if len(cuts) > 0:
        values = steps_of(rng, extent, cuts, -0.22, 0.18) * values
    return jnp.clip(values, min=-most, max=most).astype(kind)


def heavy_noise(own_key, dims, deviation, bound, pieces, heavy, held_as=jnp.bfloat16):
    entries = deviation * jax.random.normal(own_key, dims, jnp.float32)
    if pieces:
        entries = entries * steps_of(own_key, dims, pieces, -0.22, 0.18)
    return jnp.clip(raised(entries, jax.random.fold_in(own_key, 3), *heavy), -bound, bound).astype(held_as)


def setup_inputs(seed: int = 0) -> dict:
    streams_of = jax.random.split(jax.random.key(seed), 12)
    return {
        "queries": draw_queries(jax.random.fold_in(streams_of[11], 71), 0),
        "keys": draw_keys(jax.random.fold_in(streams_of[11], 71), 0),
        "values": bell_draw(streams_of[2], (FRAMES, SPATIAL, WIDTH), 1.0, 6.0, ((0, 8), (2, 4))),
        "ref_keys": draw_ref_keys(jax.random.fold_in(streams_of[11], 71), 0),
        "ref_values": bell_draw(streams_of[4], (SPATIAL, WIDTH), 1.0, 6.0, ((0, 8), (1, 4))),
        "rate_scale": jnp.clip(jnp.exp(math.log(2.0) - 3.6888794 * jax.random.uniform(streams_of[5], (HEADS,), jnp.float32) ** steps_of(streams_of[5], (HEADS,), ((0, 4),), -0.2, 0.2)), 0.05, 2.0),
        "rate_reach": jnp.clip(jnp.exp(math.log(4.0) - 3.6888794 * jax.random.uniform(streams_of[6], (HEADS,), jnp.float32) ** steps_of(streams_of[6], (HEADS,), ((0, 4),), -0.2, 0.2)), 0.1, 4.0),
        "window_start": draw_window_start(jax.random.fold_in(streams_of[11], 71), 0),
        "out_weight": heavy_noise(streams_of[8], (WIDTH, WIDTH), WIDTH ** -0.5, 0.15625, ((0, 4),), (0, 1, 4, 2.0)),
        "conv_taps": bell_draw(streams_of[9], (TAPS, WIDTH), 0.6, 3.0, ((1, 4),), jnp.float32),
        "cotangent": bell_draw(streams_of[10], (FRAMES, SPATIAL, WIDTH), 1.0, 6.0, ((0, 8), (2, 4))),
    }


def kerple_bias(rate_scale, rate_reach, starts):
    count = starts.shape[0]
    places = jnp.arange(count, dtype=jnp.int32)
    distance = jnp.abs(places[:, None] - places[None, :]).astype(jnp.float32)
    penalty = -rate_scale[:, None, None] * jnp.log1p(rate_reach[:, None, None] * distance[None])
    allowed = (places[None, :] <= places[:, None]) & (places[None, :] >= starts[:, None])
    return (penalty, allowed)

def temporal_attend(query_all, key_all, value_all, penalty, allowed):
    frame_count, positions, channels = query_all.shape
    head_count = channels // HEAD_DIM
    query_heads = query_all.reshape(frame_count, positions, head_count, HEAD_DIM)
    key_heads = key_all.reshape(frame_count, positions, head_count, HEAD_DIM)
    value_heads = value_all.reshape(frame_count, positions, head_count, HEAD_DIM)
    scores = jnp.einsum('fphd,gphd->hpfg', query_heads, key_heads) * HEAD_DIM ** (-0.5) + penalty[:, None]
    scores = jnp.where(allowed[None, None], scores, -jnp.inf)
    weights = jax.nn.softmax(scores, axis=-1)
    result = jnp.einsum('hpfg,gphd->fphd', weights, value_heads)
    return result.reshape(frame_count, positions, channels)

def ref_attend(query_all, ref_key_all, ref_value_all):
    frame_count, positions, channels = query_all.shape
    head_count = channels // HEAD_DIM
    key_heads = ref_key_all.reshape(ref_key_all.shape[0], head_count, HEAD_DIM)
    value_heads = ref_value_all.reshape(ref_value_all.shape[0], head_count, HEAD_DIM)

    def one_frame(query_frame):
        query_heads = query_frame.reshape(positions, head_count, HEAD_DIM)
        scores = jnp.einsum('shd,thd->hst', query_heads, key_heads) * HEAD_DIM ** (-0.5)
        weights = jax.nn.softmax(scores, axis=-1)
        return jnp.einsum('hst,thd->shd', weights, value_heads).reshape(positions, channels)
    return lax.map(jax.checkpoint(one_frame), query_all)

def causal_mix(extended, taps, frame_count):
    lead = taps.shape[0] - 1
    result = taps[0] * extended[lead:lead + frame_count]
    for offset in range(1, taps.shape[0]):
        result = result + taps[offset] * extended[lead - offset:lead - offset + frame_count]
    return result

def anti_mix(extended, taps, frame_count):
    result = taps[0] * extended[0:frame_count]
    for offset in range(1, taps.shape[0]):
        result = result + taps[offset] * extended[offset:offset + frame_count]
    return result

def tap_products(grad_out, extended, tap_count):
    lead = tap_count - 1
    frame_count = grad_out.shape[0]
    terms = []
    for offset in range(tap_count):
        terms.append(lax.optimization_barrier(jnp.sum(grad_out * extended[lead - offset:lead - offset + frame_count], axis=(0, 1))))
    return jnp.stack(terms)

def reference(queries, keys, values, ref_keys, ref_values, rate_scale, rate_reach, window_start, out_weight, conv_taps, cotangent):
    penalty, allowed = kerple_bias(rate_scale, rate_reach, window_start)

    def attend(query_all, key_all, value_all, ref_key_all, ref_value_all):
        return temporal_attend(query_all, key_all, value_all, penalty, allowed) + ref_attend(query_all, ref_key_all, ref_value_all)
    summed, pullback = jax.vjp(attend, queries.astype(jnp.float32), keys.astype(jnp.float32), values.astype(jnp.float32), ref_keys.astype(jnp.float32), ref_values.astype(jnp.float32))
    attended = summed.astype(jnp.bfloat16)
    attended_rows = attended.reshape(FRAMES * SPATIAL, WIDTH)
    mixed = jnp.dot(attended_rows, out_weight, preferred_element_type=jnp.float32).astype(jnp.bfloat16)
    lead = TAPS - 1
    past = jnp.concatenate([jnp.zeros((lead, SPATIAL, WIDTH), jnp.float32), mixed.reshape(FRAMES, SPATIAL, WIDTH).astype(jnp.float32)], 0)
    block_out = causal_mix(past, conv_taps, FRAMES).astype(jnp.bfloat16)
    grad_out = cotangent.astype(jnp.float32)
    future = jnp.concatenate([grad_out, jnp.zeros((lead, SPATIAL, WIDTH), jnp.float32)], 0)
    grad_mixed = anti_mix(future, conv_taps, FRAMES).astype(jnp.bfloat16)
    grad_taps = tap_products(grad_out, past, TAPS)
    grad_rows = grad_mixed.reshape(FRAMES * SPATIAL, WIDTH)
    grad_attended = lax.dot_general(grad_rows, out_weight, (((1,), (1,)), ((), ())), preferred_element_type=jnp.float32).astype(jnp.bfloat16)
    grad_weight = lax.dot_general(attended_rows, grad_rows, (((0,), (0,)), ((), ())), preferred_element_type=jnp.float32)
    grads = pullback(grad_attended.reshape(FRAMES, SPATIAL, WIDTH).astype(jnp.float32))
    return (block_out, grads[0].astype(jnp.bfloat16), grads[1].astype(jnp.bfloat16), grads[2].astype(jnp.bfloat16), grads[3], grads[4], grad_weight, grad_taps)
```

```python
import jax
import jax.numpy as jnp
from jax import lax
from jax.experimental import pallas as pl
from jax.experimental.pallas import tpu as pltpu
from jax.sharding import PartitionSpec as P

HEAD_DIM = 128
SCALE = HEAD_DIM ** (-0.5)
LOG2E = 1.4426950408889634
BLOCK = 16
HIDDEN = -1e30
CHUNKS = 1
BF16 = jnp.bfloat16
F32 = jnp.float32
ANY = pl.BlockSpec(memory_space=pl.ANY)
SMEM = pl.BlockSpec(memory_space=pltpu.SMEM)
LIMIT = pltpu.CompilerParams(vmem_limit_bytes=48 * 2**20)


def dot(a, b):
    return lax.dot_general(a, b, (((1,), (0,)), ((), ())), preferred_element_type=F32)


def dot_nt(a, b):
    return lax.dot_general(a, b, (((1,), (1,)), ((), ())), preferred_element_type=F32)


def dot_tn(a, b):
    return lax.dot_general(a, b, (((0,), (0,)), ((), ())), preferred_element_type=F32)


def run_copies(copies):
    for copy in copies:
        copy.start()
    for copy in copies:
        copy.wait()


def pack(arrays, me, count):
    frames, spatial, channels = arrays[0].shape
    held = spatial // count
    part = held // CHUNKS
    total = len(arrays)

    def kernel(me_ref, *refs):
        sources, pieces, sems = refs[:total], refs[total:-1], refs[-1]
        copies = []
        for chunk in range(CHUNKS):
            for s in range(count):
                start = pl.multiple_of((me_ref[0] ^ s) * held + chunk * part, part)
                for a in range(total):
                    copies.append(
                        pltpu.make_async_copy(
                            sources[a].at[:, pl.ds(start, part), :],
                            pieces[chunk * count + s].at[a],
                            sems.at[len(copies)],
                        )
                    )
        run_copies(copies)

    flat = pl.pallas_call(
        kernel,
        in_specs=[SMEM] + [ANY] * total,
        out_specs=[ANY] * (CHUNKS * count),
        out_shape=[jax.ShapeDtypeStruct((total, frames, part, channels), BF16)] * (CHUNKS * count),
        scratch_shapes=[pltpu.SemaphoreType.DMA((CHUNKS * count * total,))],
        cost_estimate=pl.CostEstimate(
            flops=0, bytes_accessed=4 * total * arrays[0].size, transcendentals=0
        ),
    )(me, *arrays)
    return [flat[c * count : (c + 1) * count] for c in range(CHUNKS)]


def unpack(pieces, me, count):
    total, frames, part, channels = pieces[0][0].shape
    held = part * CHUNKS
    flat = [piece for chunk in pieces for piece in chunk]

    def kernel(me_ref, *refs):
        sources, results, sems = refs[: len(flat)], refs[len(flat) : -1], refs[-1]
        copies = []
        for chunk in range(CHUNKS):
            for s in range(count):
                start = pl.multiple_of((me_ref[0] ^ s) * held + chunk * part, part)
                for a in range(total):
                    copies.append(
                        pltpu.make_async_copy(
                            sources[chunk * count + s].at[a],
                            results[a].at[:, pl.ds(start, part), :],
                            sems.at[len(copies)],
                        )
                    )
        run_copies(copies)

    return pl.pallas_call(
        kernel,
        in_specs=[SMEM] + [ANY] * len(flat),
        out_specs=[ANY] * total,
        out_shape=[jax.ShapeDtypeStruct((frames, held * count, channels), BF16)] * total,
        scratch_shapes=[pltpu.SemaphoreType.DMA((len(flat) * total,))],
        cost_estimate=pl.CostEstimate(
            flops=0, bytes_accessed=4 * len(flat) * flat[0].size, transcendentals=0
        ),
    )(me, *flat)


def swap(value, s):
    count = lax.axis_size("frame")
    return lax.ppermute(value, "frame", [(i, i ^ s) for i in range(count)])


def exchange(pieces):
    return [pieces[0]] + [swap(pieces[s], s) for s in range(1, len(pieces))]


def collect(own, count):
    even = [own] + [swap(own, s) for s in range(2, count, 2)]
    odd = swap(jnp.stack(even), 1)
    return [even[s // 2] if s % 2 == 0 else odd[s // 2] for s in range(count)]


def reduce_pieces(even, odd):
    near = swap(odd.astype(BF16), 1).astype(F32)
    sums = even + near
    total = sums[0]
    for t in range(1, even.shape[0]):
        total = total + swap(sums[t].astype(BF16), 2 * t).astype(F32)
    return total


def temporal_bias(rate_scale, rate_reach, starts, me, count):
    frames = starts.shape[0]
    local = frames // count
    places = ((me ^ jnp.arange(count, dtype=jnp.int32))[:, None] * local + jnp.arange(local)).reshape(frames)
    distance = jnp.abs(places[:, None] - places[None, :]).astype(F32)
    penalty = -rate_scale[:, None, None] * jnp.log1p(rate_reach[:, None, None] * distance[None])
    allowed = (places[:, None] <= places[None, :]) & (places[:, None] >= starts[places][None, :])
    small = jnp.where(allowed[None], penalty * LOG2E, HIDDEN)
    same = jnp.eye(BLOCK, dtype=jnp.bool_)
    wide = jnp.where(same[None, None, :, None, :], small[:, :, None, :, None], HIDDEN)
    return wide.reshape(rate_scale.shape[0], frames * BLOCK, frames * BLOCK)


def weights_of(scores):
    raised = jnp.exp2(scores - jnp.max(scores, axis=0, keepdims=True))
    return raised, 1.0 / jnp.sum(raised, axis=0, keepdims=True)


def block_rows(refs, index, at):
    parts = []
    for ref in refs:
        value = ref[index, :, at, :]
        parts.append(value.reshape(value.shape[0] * value.shape[1], HEAD_DIM))
    return jnp.concatenate(parts, axis=0)


def attend(video, refs, bias):
    count = len(video)
    _, frames, part, channels = video[0].shape
    tokens = refs[0].shape[1]
    heads = channels // HEAD_DIM
    rows = bias.shape[1]

    def kernel(*args):
        video_refs, kv_refs, bias_ref, out_ref = args[:count], args[count : 2 * count], args[-2], args[-1]
        ref_key = jnp.concatenate([r[0] for r in kv_refs], axis=0)
        ref_value_t = jnp.concatenate([r[1] for r in kv_refs], axis=0).T
        for b in range(part // BLOCK):
            at = slice(b * BLOCK, (b + 1) * BLOCK)
            query, key, value = (block_rows(video_refs, a, at) for a in range(3))
            raised, inverse = weights_of(dot_nt(key, query) * (SCALE * LOG2E) + bias_ref[0])
            total = dot(value.T, raised.astype(BF16)) * inverse
            raised, inverse = weights_of(dot_nt(ref_key, query) * (SCALE * LOG2E))
            total = total + dot(ref_value_t, raised.astype(BF16)) * inverse
            out_ref[:, :, at, :] = total.T.astype(BF16).reshape(count, frames, BLOCK, HEAD_DIM)

    all_rows = count * frames * part
    return pl.pallas_call(
        kernel,
        grid=(heads,),
        in_specs=[pl.BlockSpec((3, frames, part, HEAD_DIM), lambda h: (0, 0, 0, h))] * count
        + [pl.BlockSpec((2, tokens, HEAD_DIM), lambda h: (0, 0, h))] * count
        + [pl.BlockSpec((1, rows, rows), lambda h: (h, 0, 0))],
        out_specs=pl.BlockSpec((count, frames, part, HEAD_DIM), lambda h: (0, 0, 0, h)),
        out_shape=jax.ShapeDtypeStruct((count, frames, part, channels), BF16),
        compiler_params=LIMIT,
        cost_estimate=pl.CostEstimate(
            flops=4 * all_rows * channels * (rows + tokens * count),
            bytes_accessed=8 * all_rows * channels,
            transcendentals=all_rows * heads * (rows + tokens * count),
        ),
    )(*video, *refs, bias)


def attend_back(video, refs, bias, grad):
    count = len(video)
    _, frames, part, channels = video[0].shape
    tokens = refs[0].shape[1]
    heads = channels // HEAD_DIM
    rows = bias.shape[1]

    def kernel(*args):
        video_refs, kv_refs, bias_ref, grad_ref = (
            args[:count],
            args[count : 2 * count],
            args[2 * count],
            args[2 * count + 1],
        )
        outs = args[2 * count + 2 : 3 * count + 2]
        out_ref_key, out_ref_value = args[3 * count + 2 :]
        ref_key = jnp.concatenate([r[0] for r in kv_refs], axis=0)
        ref_value = jnp.concatenate([r[1] for r in kv_refs], axis=0)
        ref_key_t = ref_key.T

        def back(scores, value, grad_rows):
            raised, inverse = weights_of(scores)
            weights = raised * inverse
            pulled = dot_nt(value, grad_rows)
            centre = jnp.sum(weights * pulled, axis=0, keepdims=True)
            return weights.astype(BF16), (weights * (pulled - centre)).astype(BF16)

        sum_key = jnp.zeros((tokens * count, HEAD_DIM), F32)
        sum_value = jnp.zeros((tokens * count, HEAD_DIM), F32)
        for b in range(part // BLOCK):
            at = slice(b * BLOCK, (b + 1) * BLOCK)
            query, key, value = (block_rows(video_refs, a, at) for a in range(3))
            grad_rows = grad_ref[:, :, at, :].reshape(rows, HEAD_DIM)
            weights, slopes = back(
                dot_nt(key, query) * (SCALE * LOG2E) + bias_ref[0], value, grad_rows
            )
            grad_value = dot(weights, grad_rows)
            grad_key = dot(slopes, query) * SCALE
            grad_query_t = dot(key.T, slopes)
            weights, slopes = back(dot_nt(ref_key, query) * (SCALE * LOG2E), ref_value, grad_rows)
            sum_value = sum_value + dot(weights, grad_rows)
            sum_key = sum_key + dot(slopes, query)
            grad_query = (grad_query_t + dot(ref_key_t, slopes)).T * SCALE
            for a, result in enumerate((grad_query, grad_key, grad_value)):
                split = result.astype(BF16).reshape(count, frames, BLOCK, HEAD_DIM)
                for s in range(count):
                    outs[s][a, :, at, :] = split[s]
        for s in range(count):
            here = slice(s * tokens, (s + 1) * tokens)
            out_ref_key[s] = sum_key[here] * SCALE
            out_ref_value[s] = sum_value[here]

    all_rows = count * frames * part
    results = pl.pallas_call(
        kernel,
        grid=(heads,),
        in_specs=[pl.BlockSpec((3, frames, part, HEAD_DIM), lambda h: (0, 0, 0, h))] * count
        + [pl.BlockSpec((2, tokens, HEAD_DIM), lambda h: (0, 0, h))] * count
        + [
            pl.BlockSpec((1, rows, rows), lambda h: (h, 0, 0)),
            pl.BlockSpec((count, frames, part, HEAD_DIM), lambda h: (0, 0, 0, h)),
        ],
        out_specs=[pl.BlockSpec((3, frames, part, HEAD_DIM), lambda h: (0, 0, 0, h))] * count
        + [pl.BlockSpec((count, tokens, HEAD_DIM), lambda h: (0, 0, h))] * 2,
        out_shape=[jax.ShapeDtypeStruct((3, frames, part, channels), BF16)] * count
        + [jax.ShapeDtypeStruct((count, tokens, channels), F32)] * 2,
        compiler_params=LIMIT,
        cost_estimate=pl.CostEstimate(
            flops=10 * all_rows * channels * (rows + tokens * count),
            bytes_accessed=16 * all_rows * channels,
            transcendentals=all_rows * heads * (rows + tokens * count),
        ),
    )(*video, *refs, bias, grad)
    return results[:count], results[count], results[count + 1]


def mix_back(pieces, taps, me):
    count = len(pieces)
    _, frames, part, channels = pieces[0].shape
    reach = taps.shape[0]
    full = count * frames

    def kernel(me_ref, taps_ref, *refs):
        out_ref, line = refs[-2], refs[-1]
        for s in range(count):
            for u in range(frames):
                line[(me_ref[0] ^ s) * frames + u] = refs[s][0, u].astype(F32)
        for k in range(reach - 1):
            line[full + k] = jnp.zeros((part, HEAD_DIM), F32)
        for s in range(count):
            for u in range(frames):
                place = (me_ref[0] ^ s) * frames + u
                total = taps_ref[0:1, :] * line[place]
                for k in range(1, reach):
                    total = total + taps_ref[k : k + 1, :] * line[place + k]
                out_ref[s, u] = total.astype(BF16)

    return pl.pallas_call(
        kernel,
        grid=(channels // HEAD_DIM,),
        in_specs=[SMEM, pl.BlockSpec((reach, HEAD_DIM), lambda h: (0, h))]
        + [pl.BlockSpec((1, frames, part, HEAD_DIM), lambda h: (0, 0, 0, h))] * count,
        out_specs=pl.BlockSpec((count, frames, part, HEAD_DIM), lambda h: (0, 0, 0, h)),
        out_shape=jax.ShapeDtypeStruct((count, frames, part, channels), BF16),
        scratch_shapes=[pltpu.VMEM((full + reach - 1, part, HEAD_DIM), F32)],
        compiler_params=LIMIT,
        cost_estimate=pl.CostEstimate(
            flops=6 * full * part * channels, bytes_accessed=4 * full * part * channels, transcendentals=0
        ),
    )(me, taps, *pieces)


def mix(terms, pieces, taps, me):
    count = len(pieces)
    _, frames, part, channels = pieces[0].shape
    reach = taps.shape[0]
    lead = reach - 1
    full = count * frames
    total_terms = len(terms)

    def kernel(me_ref, taps_ref, *refs):
        term_refs, cot_refs = refs[:total_terms], refs[total_terms : total_terms + count]
        outs, taps_out, line = refs[total_terms + count : -2], refs[-2], refs[-1]
        for k in range(lead):
            line[k] = jnp.zeros((part, HEAD_DIM), F32)
        for s in range(count):
            for u in range(frames):
                value = term_refs[0][s, u].astype(F32)
                for term in term_refs[1:]:
                    value = value + term[s, u].astype(F32)
                line[(me_ref[0] ^ s) * frames + u + lead] = value.astype(BF16).astype(F32)
        sums = [jnp.zeros((part, HEAD_DIM), F32) for _ in range(reach)]
        for s in range(count):
            for u in range(frames):
                place = (me_ref[0] ^ s) * frames + u + lead
                cot = cot_refs[s][0, u].astype(F32)
                total = jnp.zeros((part, HEAD_DIM), F32)
                for k in range(reach):
                    past = line[place - k]
                    total = total + taps_ref[k : k + 1, :] * past
                    sums[k] = sums[k] + cot * past
                outs[s][0, u] = total.astype(BF16)
        for k in range(reach):
            taps_out[k : k + 1, :] = jnp.sum(sums[k], axis=0, keepdims=True)

    results = pl.pallas_call(
        kernel,
        grid=(channels // HEAD_DIM,),
        in_specs=[SMEM, pl.BlockSpec((reach, HEAD_DIM), lambda h: (0, h))]
        + [pl.BlockSpec((count, frames, part, HEAD_DIM), lambda h: (0, 0, 0, h))] * total_terms
        + [pl.BlockSpec((1, frames, part, HEAD_DIM), lambda h: (0, 0, 0, h))] * count,
        out_specs=[pl.BlockSpec((1, frames, part, HEAD_DIM), lambda h: (0, 0, 0, h))] * count
        + [pl.BlockSpec((reach, HEAD_DIM), lambda h: (0, h))],
        out_shape=[jax.ShapeDtypeStruct((1, frames, part, channels), BF16)] * count
        + [jax.ShapeDtypeStruct((reach, channels), F32)],
        scratch_shapes=[pltpu.VMEM((full + lead, part, HEAD_DIM), F32)],
        compiler_params=LIMIT,
        cost_estimate=pl.CostEstimate(
            flops=12 * full * part * channels, bytes_accessed=10 * full * part * channels, transcendentals=0
        ),
    )(me, taps, *terms, *pieces)
    return results[:count], results[count]


def per_device(
    queries,
    keys,
    values,
    ref_keys,
    ref_values,
    rate_scale,
    rate_reach,
    window_start,
    out_weight,
    conv_taps,
    cotangent,
):
    frames, spatial, channels = queries.shape
    width = out_weight.shape[1]
    count, depth = lax.axis_size("frame"), lax.axis_size("head")
    place, level = lax.axis_index("frame"), lax.axis_index("head")
    me = place.reshape(1).astype(jnp.int32)
    part = spatial // count // CHUNKS
    rows = count * frames * part
    shape = (count, frames, part, channels)

    def weight_block(j):
        return lax.dynamic_slice_in_dim(out_weight, jnp.clip(j, 0, depth - 1) * channels, channels, 1)

    cot = [exchange(chunk) for chunk in pack([cotangent], me, count)]
    video = [exchange(chunk) for chunk in pack([queries, keys, values], me, count)]
    refs = collect(jnp.stack([ref_keys, ref_values]), count)
    bias = temporal_bias(rate_scale, rate_reach, window_start, place, count)

    blocks = []
    for c in range(CHUNKS):
        own = mix_back(cot[c], conv_taps, me).reshape(rows, channels)
        arrived = [(own, level)]
        up = down = own
        for s in range(1, depth):
            up = lax.ppermute(up, "head", [(i, i + 1) for i in range(s - 1, depth - 1)])
            down = lax.ppermute(down, "head", [(i, i - 1) for i in range(1, depth - s + 1)])
            if 2 * s < depth:
                arrived += [(up, level - s), (down, level + s)]
            else:
                arrived.append((jnp.where(level >= s, up, down), jnp.where(level >= s, level - s, level + s)))
        blocks.append(arrived)

    attended = [attend(video[c], refs, bias).reshape(rows, channels) for c in range(CHUNKS)]

    out_pieces, taps_sum = [], 0.0
    for c in range(CHUNKS):
        shares = dot(attended[c], out_weight).astype(BF16)

        def share(j):
            return lax.dynamic_slice_in_dim(shares, jnp.clip(j, 0, depth - 1) * channels, channels, 1)

        up = down = None
        for s in range(1, depth):
            far = depth - s
            send_up, send_down = share(level + far), share(level - far)
            if s > 1:
                send_up = (send_up.astype(F32) + up.astype(F32)).astype(BF16)
                send_down = (send_down.astype(F32) + down.astype(F32)).astype(BF16)
            up = lax.ppermute(send_up, "head", [(i, i + 1) for i in range(depth - far)])
            down = lax.ppermute(send_down, "head", [(i, i - 1) for i in range(far, depth)])
        terms = [t.reshape(shape) for t in (share(level), up, down)]
        pieces, taps_part = mix(terms, cot[c], conv_taps, me)
        out_pieces.append(exchange(pieces))
        taps_sum = taps_sum + taps_part

    slots = jnp.zeros((3 * depth - 2, channels, channels), F32)
    for step in range(len(blocks[0])):
        term = sum(dot_tn(attended[c], blocks[c][step][0]) for c in range(CHUNKS))
        slots = lax.dynamic_update_slice_in_dim(slots, term[None], blocks[0][step][1] + depth - 1, 0)
    columns = width // count
    per_block = channels // columns

    def weight_piece(s):
        target = place ^ s
        return lax.dynamic_slice(
            slots,
            (depth - 1 + target // per_block, 0, (target % per_block) * columns),
            (1, channels, columns),
        )[0]

    grad_weight = reduce_pieces(
        jnp.stack([weight_piece(s) for s in range(0, count, 2)]),
        jnp.stack([weight_piece(s) for s in range(1, count, 2)]),
    )

    grad_pieces, ref_key_sum, ref_value_sum = [], 0.0, 0.0
    for c in range(CHUNKS):
        total = sum(dot_nt(block, weight_block(j)) for block, j in blocks[c])
        pieces, ref_key_part, ref_value_part = attend_back(
            video[c], refs, bias, total.astype(BF16).reshape(shape)
        )
        grad_pieces.append(exchange(pieces))
        ref_key_sum = ref_key_sum + ref_key_part
        ref_value_sum = ref_value_sum + ref_value_part

    ref_sum = jnp.stack([ref_key_sum, ref_value_sum], axis=1)
    ref_grads = reduce_pieces(ref_sum[0::2], ref_sum[1::2])

    step = 1
    while step < count:
        taps_sum = taps_sum + swap(taps_sum, step)
        step *= 2

    (block_out,) = unpack(out_pieces, me, count)
    grad_queries, grad_keys, grad_values = unpack(grad_pieces, me, count)
    return (
        block_out,
        grad_queries,
        grad_keys,
        grad_values,
        ref_grads[0],
        ref_grads[1],
        grad_weight,
        taps_sum,
    )


def solution(mesh):
    video = P("frame", None, "head")
    tokens = P("frame", "head")
    return jax.shard_map(
        per_device,
        mesh=mesh,
        in_specs=(
            video,
            video,
            video,
            tokens,
            tokens,
            P("head"),
            P("head"),
            P(),
            P("head", None),
            P(None, "head"),
            video,
        ),
        out_specs=(video, video, video, video, tokens, tokens, P("head", "frame"), P(None, "head")),
        check_vma=False,
    )
```

```python
import jax
import jax.numpy as jnp
from jax import lax
from jax.experimental import pallas as pl
from jax.experimental.pallas import tpu as pltpu
from jax.sharding import PartitionSpec as P

HEAD_DIM = 128
SCALE = HEAD_DIM ** (-0.5)
LOG2E = 1.4426950408889634
BLOCK = 16
HIDDEN = -1e30
CHUNKS = 1
BF16 = jnp.bfloat16
F32 = jnp.float32
ANY = pl.BlockSpec(memory_space=pl.ANY)
SMEM = pl.BlockSpec(memory_space=pltpu.SMEM)
LIMIT = pltpu.CompilerParams(vmem_limit_bytes=48 * 2**20)


def dot(a, b):
    return lax.dot_general(a, b, (((1,), (0,)), ((), ())), preferred_element_type=F32)


def dot_nt(a, b):
    return lax.dot_general(a, b, (((1,), (1,)), ((), ())), preferred_element_type=F32)


def dot_tn(a, b):
    return lax.dot_general(a, b, (((0,), (0,)), ((), ())), preferred_element_type=F32)


def swap(value, s):
    count = lax.axis_size("frame")
    return lax.ppermute(value, "frame", [(i, i ^ s) for i in range(count)])


def collect(own, count):
    even = jnp.stack([own] + [swap(own, s) for s in range(2, count, 2)])
    return even, swap(even, 1)


def reduce_pieces(even, odd):
    sums = even + swap(odd.astype(BF16), 1).astype(F32)
    total = sums[0]
    for t in range(1, even.shape[0]):
        total = total + swap(sums[t].astype(BF16), 2 * t).astype(F32)
    return total


def to_positions(arrays, count):
    frames, spatial, channels = arrays[0].shape
    split = [a.reshape(frames, count, 1, spatial // count, channels).transpose(1, 2, 0, 3, 4) for a in arrays]
    return jnp.concatenate(split, axis=1)


def travel(value):
    return lax.all_to_all(value, "frame", split_axis=0, concat_axis=0, tiled=True)


def to_frames(value):
    count, total, frames, part, channels = value.shape
    return value.transpose(1, 2, 0, 3, 4).reshape(total, frames, count * part, channels)


def temporal_bias(rate_scale, rate_reach, starts):
    places = jnp.arange(starts.shape[0], dtype=jnp.int32)
    distance = jnp.abs(places[:, None] - places[None, :]).astype(F32)
    penalty = -rate_scale[:, None, None] * jnp.log1p(rate_reach[:, None, None] * distance[None])
    allowed = (places[:, None] <= places[None, :]) & (places[:, None] >= starts[None, :])
    return jnp.repeat(jnp.where(allowed[None], penalty * LOG2E, HIDDEN), BLOCK, axis=2)


def widen(bias):
    frames, rows = bias.shape
    wide = jnp.broadcast_to(bias[:, None, :], (frames, BLOCK, rows)).reshape(rows, rows)
    key_place = lax.broadcasted_iota(jnp.int32, (rows, rows), 0) % BLOCK
    query_place = lax.broadcasted_iota(jnp.int32, (rows, rows), 1) % BLOCK
    return jnp.where(key_place == query_place, wide, HIDDEN)


def weights_of(scores):
    raised = jnp.exp2(scores - jnp.max(scores, axis=0, keepdims=True))
    return raised, 1.0 / jnp.sum(raised, axis=0, keepdims=True)


def stacked(ref, index):
    value = ref[:, index]
    return value.reshape(value.shape[0] * value.shape[1], HEAD_DIM)


def attend(video, even, odd, bias):
    count, _, frames, part, channels = video.shape
    tokens = even.shape[2]
    heads = channels // HEAD_DIM
    rows = count * frames * BLOCK

    def kernel(video_ref, even_ref, odd_ref, bias_ref, out_ref):
        ref_key = jnp.concatenate([stacked(even_ref, 0), stacked(odd_ref, 0)], axis=0)
        ref_value_t = jnp.concatenate([stacked(even_ref, 1), stacked(odd_ref, 1)], axis=0).T
        wide = widen(bias_ref[0])
        for b in range(part // BLOCK):
            at = slice(b * BLOCK, (b + 1) * BLOCK)
            query, key, value = (video_ref[:, a, :, at, :].reshape(rows, HEAD_DIM) for a in range(3))
            raised, inverse = weights_of(dot_nt(key, query) * (SCALE * LOG2E) + wide)
            total = dot(value.T, raised.astype(BF16)) * inverse
            raised, inverse = weights_of(dot_nt(ref_key, query) * (SCALE * LOG2E))
            total = total + dot(ref_value_t, raised.astype(BF16)) * inverse
            out_ref[:, :, at, :] = total.T.astype(BF16).reshape(count, frames, BLOCK, HEAD_DIM)

    all_rows = count * frames * part
    return pl.pallas_call(
        kernel,
        grid=(heads,),
        in_specs=[pl.BlockSpec((count, 3, frames, part, HEAD_DIM), lambda h: (0, 0, 0, 0, h))]
        + [pl.BlockSpec((count // 2, 2, tokens, HEAD_DIM), lambda h: (0, 0, 0, h))] * 2
        + [pl.BlockSpec((1, count * frames, rows), lambda h: (h, 0, 0))],
        out_specs=pl.BlockSpec((count, frames, part, HEAD_DIM), lambda h: (0, 0, 0, h)),
        out_shape=jax.ShapeDtypeStruct((count, frames, part, channels), BF16),
        compiler_params=LIMIT,
        cost_estimate=pl.CostEstimate(
            flops=4 * all_rows * channels * (rows + tokens * count),
            bytes_accessed=8 * all_rows * channels,
            transcendentals=all_rows * heads * (rows + tokens * count),
        ),
    )(video, even, odd, bias)


def attend_back(video, even, odd, bias, grad):
    count, _, frames, part, channels = video.shape
    tokens = even.shape[2]
    heads = channels // HEAD_DIM
    rows = count * frames * BLOCK
    half = tokens * count // 2

    def kernel(video_ref, even_ref, odd_ref, bias_ref, grad_ref, out_ref, even_out, odd_out):
        ref_key = jnp.concatenate([stacked(even_ref, 0), stacked(odd_ref, 0)], axis=0)
        ref_value = jnp.concatenate([stacked(even_ref, 1), stacked(odd_ref, 1)], axis=0)
        ref_key_t = ref_key.T
        wide = widen(bias_ref[0])

        def back(scores, value, grad_rows):
            raised, inverse = weights_of(scores)
            weights = raised * inverse
            pulled = dot_nt(value, grad_rows)
            centre = jnp.sum(weights * pulled, axis=0, keepdims=True)
            return weights.astype(BF16), (weights * (pulled - centre)).astype(BF16)

        sums = [jnp.zeros((2 * half, HEAD_DIM), F32) for _ in range(2)]
        for b in range(part // BLOCK):
            at = slice(b * BLOCK, (b + 1) * BLOCK)
            query, key, value = (video_ref[:, a, :, at, :].reshape(rows, HEAD_DIM) for a in range(3))
            grad_rows = grad_ref[:, :, at, :].reshape(rows, HEAD_DIM)
            weights, slopes = back(dot_nt(key, query) * (SCALE * LOG2E) + wide, value, grad_rows)
            grad_value = dot(weights, grad_rows)
            grad_key = dot(slopes, query) * SCALE
            grad_query_t = dot(key.T, slopes)
            weights, slopes = back(dot_nt(ref_key, query) * (SCALE * LOG2E), ref_value, grad_rows)
            sums[0] = sums[0] + dot(slopes, query)
            sums[1] = sums[1] + dot(weights, grad_rows)
            grad_query = (grad_query_t + dot(ref_key_t, slopes)).T * SCALE
            for a, result in enumerate((grad_query, grad_key, grad_value)):
                out_ref[:, a, :, at, :] = result.astype(BF16).reshape(count, frames, BLOCK, HEAD_DIM)
        sums[0] = sums[0] * SCALE
        for a in range(2):
            even_out[:, a] = sums[a][:half].reshape(count // 2, tokens, HEAD_DIM)
            odd_out[:, a] = sums[a][half:].reshape(count // 2, tokens, HEAD_DIM)

    all_rows = count * frames * part
    video_spec = pl.BlockSpec((count, 3, frames, part, HEAD_DIM), lambda h: (0, 0, 0, 0, h))
    ref_specs = [pl.BlockSpec((count // 2, 2, tokens, HEAD_DIM), lambda h: (0, 0, 0, h))] * 2
    return pl.pallas_call(
        kernel,
        grid=(heads,),
        in_specs=[
            video_spec,
            *ref_specs,
            pl.BlockSpec((1, count * frames, rows), lambda h: (h, 0, 0)),
            pl.BlockSpec((count, frames, part, HEAD_DIM), lambda h: (0, 0, 0, h)),
        ],
        out_specs=[video_spec, *ref_specs],
        out_shape=[jax.ShapeDtypeStruct(video.shape, BF16)]
        + [jax.ShapeDtypeStruct(even.shape, F32)] * 2,
        compiler_params=LIMIT,
        cost_estimate=pl.CostEstimate(
            flops=10 * all_rows * channels * (rows + tokens * count),
            bytes_accessed=16 * all_rows * channels,
            transcendentals=all_rows * heads * (rows + tokens * count),
        ),
    )(video, even, odd, bias, grad)


def mix_back(cot, taps):
    full, part, channels = cot.shape
    reach = taps.shape[0]

    def kernel(taps_ref, cot_ref, out_ref):
        line = [cot_ref[f].astype(F32) for f in range(full)]
        for f in range(full):
            total = taps_ref[0:1, :] * line[f]
            for k in range(1, min(reach, full - f)):
                total = total + taps_ref[k : k + 1, :] * line[f + k]
            out_ref[f] = total.astype(BF16)

    block = pl.BlockSpec((full, part, HEAD_DIM), lambda h: (0, 0, h))
    return pl.pallas_call(
        kernel,
        grid=(channels // HEAD_DIM,),
        in_specs=[pl.BlockSpec((reach, HEAD_DIM), lambda h: (0, h)), block],
        out_specs=block,
        out_shape=jax.ShapeDtypeStruct(cot.shape, BF16),
        compiler_params=LIMIT,
        cost_estimate=pl.CostEstimate(flops=6 * cot.size, bytes_accessed=4 * cot.size, transcendentals=0),
    )(taps, cot)


def mix(terms, cot, taps):
    full, part, channels = cot.shape
    reach = taps.shape[0]
    total_terms = len(terms)

    def kernel(taps_ref, *refs):
        cot_ref, out_ref, taps_out = refs[total_terms:]
        line = []
        sums = [jnp.zeros((part, HEAD_DIM), F32) for _ in range(reach)]
        for f in range(full):
            value = refs[0][f].astype(F32)
            for term in refs[1:total_terms]:
                value = value + term[f].astype(F32)
            line.append(value.astype(BF16).astype(F32))
            cot_line = cot_ref[f].astype(F32)
            total = jnp.zeros((part, HEAD_DIM), F32)
            for k in range(min(reach, f + 1)):
                total = total + taps_ref[k : k + 1, :] * line[f - k]
                sums[k] = sums[k] + cot_line * line[f - k]
            out_ref[f] = total.astype(BF16)
        for k in range(reach):
            taps_out[k : k + 1, :] = jnp.sum(sums[k], axis=0, keepdims=True)

    block = pl.BlockSpec((full, part, HEAD_DIM), lambda h: (0, 0, h))
    taps_block = pl.BlockSpec((reach, HEAD_DIM), lambda h: (0, h))
    return pl.pallas_call(
        kernel,
        grid=(channels // HEAD_DIM,),
        in_specs=[taps_block] + [block] * (total_terms + 1),
        out_specs=[block, taps_block],
        out_shape=[jax.ShapeDtypeStruct(cot.shape, BF16), jax.ShapeDtypeStruct(taps.shape, F32)],
        compiler_params=LIMIT,
        cost_estimate=pl.CostEstimate(flops=12 * cot.size, bytes_accessed=10 * cot.size, transcendentals=0),
    )(taps, *terms, cot)


def weight_terms(attended, blocks, level, count):
    depth = lax.axis_size("head")
    chunks = len(attended)
    rows, channels = attended[0].shape
    parts = count // depth
    columns = channels // parts
    offsets = sorted(blocks[0])

    def kernel(level_ref, *refs):
        held = refs[:chunks]
        sources = [
            {d: refs[chunks + c * len(offsets) + k] for k, d in enumerate(offsets)} for c in range(chunks)
        ]
        out_ref, buffer, turned, sems = refs[chunks + chunks * len(offsets) :]
        j = pl.program_id(0)

        def fetch(target, slot):
            for d in offsets:

                @pl.when(target - level_ref[0] == d)
                def _():
                    for c in range(chunks):
                        pltpu.make_async_copy(sources[c][d], buffer.at[slot, c], sems.at[slot, c]).start()

        @pl.when(j == 0)
        def _():
            fetch(j, 0)
            for c in range(chunks):
                turned[c] = held[c][...].T

        @pl.when(j + 1 < depth)
        def _():
            fetch(j + 1, (j + 1) % 2)

        total = None
        for c in range(chunks):
            pltpu.make_async_copy(sources[c][0], buffer.at[j % 2, c], sems.at[j % 2, c]).wait()
            term = dot(turned[c], buffer[j % 2, c])
            total = term if total is None else total + term
        for p in range(parts):
            out_ref[0, p] = total[:, p * columns : (p + 1) * columns].astype(BF16)

    flat = [blocks[c][d] for c in range(chunks) for d in offsets]
    return pl.pallas_call(
        kernel,
        grid=(depth,),
        in_specs=[SMEM]
        + [pl.BlockSpec((rows, channels), lambda j: (0, 0))] * chunks
        + [ANY] * len(flat),
        out_specs=pl.BlockSpec((1, parts, channels, columns), lambda j: (j, 0, 0, 0)),
        out_shape=jax.ShapeDtypeStruct((depth, parts, channels, columns), BF16),
        scratch_shapes=[
            pltpu.VMEM((2, chunks, rows, channels), BF16),
            pltpu.VMEM((chunks, channels, rows), BF16),
            pltpu.SemaphoreType.DMA((2, chunks)),
        ],
        compiler_params=LIMIT,
        cost_estimate=pl.CostEstimate(
            flops=2 * chunks * rows * channels * channels * depth,
            bytes_accessed=4 * chunks * rows * channels * depth,
            transcendentals=0,
        ),
    )(level.reshape(1).astype(jnp.int32), *attended, *flat)


def after(value, *others):
    return lax.optimization_barrier((value, *others))[0]


def per_device(
    queries,
    keys,
    values,
    ref_keys,
    ref_values,
    rate_scale,
    rate_reach,
    window_start,
    out_weight,
    conv_taps,
    cotangent,
):
    frames, spatial, channels = queries.shape
    width = out_weight.shape[1]
    count, depth = lax.axis_size("frame"), lax.axis_size("head")
    place, level = lax.axis_index("frame"), lax.axis_index("head")
    part = spatial // count // CHUNKS
    rows = count * frames * part
    line_shape = (count * frames, part, channels)

    def chunk_of(array, c):
        return lax.slice_in_dim(array, c * (spatial // CHUNKS), (c + 1) * (spatial // CHUNKS), axis=1)

    def weight_block(j):
        return lax.dynamic_slice_in_dim(out_weight, jnp.clip(j, 0, depth - 1) * channels, channels, 1)

    even, odd = collect(jnp.stack([ref_keys, ref_values]), count)
    bias = temporal_bias(rate_scale, rate_reach, window_start)

    cot, video = [], []
    for c in range(CHUNKS):
        packed = to_positions([chunk_of(cotangent, c)], count)
        if c > 0:
            packed = after(packed, video[-1])
        cot.append(travel(packed).reshape(line_shape))
        packed = to_positions([chunk_of(a, c) for a in (queries, keys, values)], count)
        video.append(travel(after(packed, cot[-1])))

    blocks, totals = [], []
    for c in range(CHUNKS):
        own = mix_back(cot[c], conv_taps).reshape(rows, channels)
        arrived = {0: own}
        total = dot_nt(own, weight_block(level))
        up = down = own
        for s in range(1, depth):
            up = lax.ppermute(up, "head", [(i, i + 1) for i in range(s - 1, depth - 1)])
            down = lax.ppermute(down, "head", [(i, i - 1) for i in range(1, depth - s + 1)])
            arrived[-s], arrived[s] = up, down
            if 2 * s < depth:
                total = total + dot_nt(up, weight_block(level - s)) + dot_nt(down, weight_block(level + s))
            else:
                below = level >= s
                total = total + dot_nt(
                    jnp.where(below, up, down), weight_block(jnp.where(below, level - s, level + s))
                )
        blocks.append(arrived)
        totals.append(total.astype(BF16).reshape(count, frames, part, channels))

    attended = [attend(video[c], even, odd, bias).reshape(rows, channels) for c in range(CHUNKS)]

    outs, taps_sum = [], 0.0
    for c in range(CHUNKS):
        shares = dot(attended[c], out_weight).astype(BF16)

        def share(j):
            return lax.dynamic_slice_in_dim(shares, jnp.clip(j, 0, depth - 1) * channels, channels, 1)

        up = down = None
        for s in range(1, depth):
            far = depth - s
            send_up, send_down = share(level + far), share(level - far)
            if s > 1:
                send_up = (send_up.astype(F32) + up.astype(F32)).astype(BF16)
                send_down = (send_down.astype(F32) + down.astype(F32)).astype(BF16)
            up = lax.ppermute(send_up, "head", [(i, i + 1) for i in range(depth - far)])
            down = lax.ppermute(send_down, "head", [(i, i - 1) for i in range(far, depth)])
        out, taps_part = mix([t.reshape(line_shape) for t in (share(level), up, down)], cot[c], conv_taps)
        outs.append(to_frames(travel(out.reshape(count, 1, frames, part, channels))))
        taps_sum = taps_sum + taps_part

    terms = weight_terms(attended, blocks, level, count)
    columns = terms.shape[3]
    by_chip = terms.reshape(count // 2, 2, channels, columns)
    core = place % 2
    near = swap(lax.dynamic_index_in_dim(by_chip, 1 - core, 1, keepdims=False), 1)
    sums = lax.dynamic_index_in_dim(by_chip, core, 1, keepdims=False).astype(F32) + near.astype(F32)
    groups = [list(range(k, count, 2)) for k in range(2)]
    far = lax.all_to_all(
        sums.astype(BF16), "frame", split_axis=0, concat_axis=0, axis_index_groups=groups, tiled=True
    )
    grad_weight = jnp.sum(far.astype(F32), axis=0)

    grads, ref_even, ref_odd = [], 0.0, 0.0
    for c in range(CHUNKS):
        back, even_part, odd_part = attend_back(video[c], even, odd, bias, totals[c])
        grads.append(to_frames(travel(back)))
        ref_even, ref_odd = ref_even + even_part, ref_odd + odd_part
    ref_grads = reduce_pieces(ref_even, ref_odd)

    step = 1
    while step < count:
        taps_sum = taps_sum + swap(taps_sum, step)
        step *= 2

    block_out = jnp.concatenate([out[0] for out in outs], axis=1)
    grad_queries, grad_keys, grad_values = (
        jnp.concatenate([grad[a] for grad in grads], axis=1) for a in range(3)
    )
    return (
        block_out,
        grad_queries,
        grad_keys,
        grad_values,
        ref_grads[0],
        ref_grads[1],
        grad_weight,
        taps_sum,
    )


def solution(mesh):
    video = P("frame", None, "head")
    tokens = P("frame", "head")
    return jax.shard_map(
        per_device,
        mesh=mesh,
        in_specs=(
            video,
            video,
            video,
            tokens,
            tokens,
            P("head"),
            P("head"),
            P(),
            P("head", None),
            P(None, "head"),
            video,
        ),
        out_specs=(video, video, video, video, tokens, tokens, P("head", "frame"), P(None, "head")),
        check_vma=False,
    )
```

```python
import jax
import jax.numpy as jnp
from jax import lax
from jax.experimental import pallas as pl
from jax.experimental.pallas import tpu as pltpu
from jax.sharding import PartitionSpec as P

HEAD_DIM = 128
SCALE = HEAD_DIM ** (-0.5)
LOG2E = 1.4426950408889634
BLOCK = 16
HIDDEN = -1e30
ROW_TILE = 256
VMEM = 24
COST = 1.15e9
CHUNKS = 2
BF16 = jnp.bfloat16
F32 = jnp.float32
ANY = pl.BlockSpec(memory_space=pl.ANY)
SMEM = pl.BlockSpec(memory_space=pltpu.SMEM)
LIMIT = pltpu.CompilerParams(vmem_limit_bytes=VMEM * 2**20)


def lasting(us):
    return pl.CostEstimate(flops=int(us * COST), bytes_accessed=0, transcendentals=0)


def dot(a, b):
    return lax.dot_general(a, b, (((1,), (0,)), ((), ())), preferred_element_type=F32)


def dot_nt(a, b):
    return lax.dot_general(a, b, (((1,), (1,)), ((), ())), preferred_element_type=F32)


def dot_tn(a, b):
    return lax.dot_general(a, b, (((0,), (0,)), ((), ())), preferred_element_type=F32)


def swap(value, s):
    count = lax.axis_size("frame")
    return lax.ppermute(value, "frame", [(i, i ^ s) for i in range(count)])


def collect(own, count, deps):
    pieces = [own] + [swap(own, s) for s in range(2, count, 2)]

    def kernel(*refs):
        for t in range(len(pieces)):
            refs[-1][t] = refs[t][...]

    even = pl.pallas_call(
        kernel,
        in_specs=[pl.BlockSpec(memory_space=pltpu.VMEM)] * len(pieces) + [ANY] * len(deps),
        out_specs=pl.BlockSpec(memory_space=pltpu.VMEM),
        out_shape=jax.ShapeDtypeStruct((len(pieces), *own.shape), own.dtype),
        compiler_params=LIMIT,
        cost_estimate=lasting(1.2),
    )(*pieces, *deps)
    return even, swap(even, 1)


def reduce_pieces(even, odd, deps):
    sums = after(even, *deps) + swap(odd.astype(BF16), 1).astype(F32)
    total = sums[0]
    for t in range(1, even.shape[0]):
        total = total + swap(sums[t].astype(BF16), 2 * t).astype(F32)
    return total


def to_positions(arrays, chunk, count):
    frames, spatial, channels = arrays[0].shape
    size = spatial // CHUNKS
    split = [
        lax.slice_in_dim(a, chunk * size, (chunk + 1) * size, axis=1)
        .reshape(frames, count, 1, size // count, channels)
        .transpose(1, 2, 0, 3, 4)
        for a in arrays
    ]
    return jnp.concatenate(split, axis=1)


def after(value, *others):
    return lax.optimization_barrier((value, *others))[0]


def travel(value):
    return lax.all_to_all(value, "frame", split_axis=0, concat_axis=0, tiled=True)


def to_frames(values):
    count, frames, part, channels = values[0].shape
    return jnp.concatenate(
        [v.transpose(1, 0, 2, 3).reshape(frames, count * part, channels) for v in values], axis=1
    )


def temporal_bias(rate_scale, rate_reach, starts):
    places = jnp.arange(starts.shape[0], dtype=jnp.int32)
    distance = jnp.abs(places[:, None] - places[None, :]).astype(F32)
    penalty = -rate_scale[:, None, None] * jnp.log1p(rate_reach[:, None, None] * distance[None])
    allowed = (places[:, None] <= places[None, :]) & (places[:, None] >= starts[None, :])
    return jnp.repeat(jnp.where(allowed[None], penalty * LOG2E, HIDDEN), BLOCK, axis=2)


def widen(bias):
    frames, rows = bias.shape
    wide = jnp.broadcast_to(bias[:, None, :], (frames, BLOCK, rows)).reshape(rows, rows)
    key_place = lax.broadcasted_iota(jnp.int32, (rows, rows), 0) % BLOCK
    query_place = lax.broadcasted_iota(jnp.int32, (rows, rows), 1) % BLOCK
    return jnp.where(key_place == query_place, wide, HIDDEN)


def weights_of(scores):
    raised = jnp.exp2(scores - jnp.max(scores, axis=0, keepdims=True))
    return raised, 1.0 / jnp.sum(raised, axis=0, keepdims=True)


def stacked(ref, index):
    value = ref[:, index]
    return value.reshape(value.shape[0] * value.shape[1], HEAD_DIM)


def attend(video, even, odd, bias, deps=()):
    count, _, frames, part, channels = video.shape
    tokens = even.shape[2]
    heads = channels // HEAD_DIM
    rows = count * frames * BLOCK
    number = part // BLOCK
    all_tokens = tokens * count

    def kernel(video_ref, even_ref, odd_ref, bias_ref, *rest):
        out_ref, near_ref, far_ref, inverse_ref, parts_ref = rest[-5:]
        ref_key = jnp.concatenate([stacked(even_ref, 0), stacked(odd_ref, 0)], axis=0)
        ref_value_t = jnp.concatenate([stacked(even_ref, 1), stacked(odd_ref, 1)], axis=0).T
        wide = widen(bias_ref[0])
        for b in range(number):
            at = slice(b * BLOCK, (b + 1) * BLOCK)
            query, key, value = (video_ref[:, a, :, at, :].reshape(rows, HEAD_DIM) for a in range(3))
            total = None
            for k, (scores, value_t, keep) in enumerate(
                (
                    (dot_nt(key, query) * (SCALE * LOG2E) + wide, value.T, near_ref),
                    (dot_nt(ref_key, query) * (SCALE * LOG2E), ref_value_t, far_ref),
                )
            ):
                raised, inverse = weights_of(scores)
                raised = raised.astype(BF16)
                keep[0, b] = raised
                inverse_ref[0, b, k : k + 1, :] = inverse
                term = dot(value_t, raised) * inverse
                parts_ref[0, b, k] = term.astype(BF16)
                total = term if total is None else total + term
            out_ref[:, :, at, :] = total.T.astype(BF16).reshape(count, frames, BLOCK, HEAD_DIM)

    all_rows = count * frames * part
    saved = [
        ((number, rows, rows), BF16),
        ((number, all_tokens, rows), BF16),
        ((number, 2, rows), F32),
        ((number, 2, HEAD_DIM, rows), BF16),
    ]
    return pl.pallas_call(
        kernel,
        grid=(heads,),
        in_specs=[pl.BlockSpec((count, 3, frames, part, HEAD_DIM), lambda h: (0, 0, 0, 0, h))]
        + [pl.BlockSpec((count // 2, 2, tokens, HEAD_DIM), lambda h: (0, 0, 0, h))] * 2
        + [pl.BlockSpec((1, count * frames, rows), lambda h: (h, 0, 0))]
        + [ANY] * len(deps),
        out_specs=[pl.BlockSpec((count, frames, part, HEAD_DIM), lambda h: (0, 0, 0, h))]
        + [by_head(shape) for shape, _ in saved],
        out_shape=[jax.ShapeDtypeStruct((count, frames, part, channels), BF16)]
        + [jax.ShapeDtypeStruct((heads, *shape), kind) for shape, kind in saved],
        compiler_params=LIMIT,
        cost_estimate=lasting(8),
    )(video, even, odd, bias, *deps)


def by_head(shape):
    return pl.BlockSpec((1, *shape), lambda h: (h,) + (0,) * len(shape))


def attend_back(video, even, odd, saved, grad, deps=()):
    count, _, frames, part, channels = video.shape
    tokens = even.shape[2]
    heads = channels // HEAD_DIM
    rows = count * frames * BLOCK
    half = tokens * count // 2

    def kernel(video_ref, even_ref, odd_ref, near_ref, far_ref, inverse_ref, parts_ref, grad_ref, *rest):
        out_ref, even_out, odd_out = rest[-3:]
        ref_key = jnp.concatenate([stacked(even_ref, 0), stacked(odd_ref, 0)], axis=0)
        ref_value = jnp.concatenate([stacked(even_ref, 1), stacked(odd_ref, 1)], axis=0)
        ref_key_t = ref_key.T
        sums = [None, None]
        for b in range(part // BLOCK):
            at = slice(b * BLOCK, (b + 1) * BLOCK)
            query, key, value = (video_ref[:, a, :, at, :].reshape(rows, HEAD_DIM) for a in range(3))
            grad_t = grad_ref[:, :, at, :].reshape(rows, HEAD_DIM).T.astype(F32)
            results = []
            for k, (raised, keys_t, values) in enumerate(
                ((near_ref[0, b], key.T, value), (far_ref[0, b], ref_key_t, ref_value))
            ):
                inverse = inverse_ref[0, b, k : k + 1, :]
                scaled_t = (grad_t * inverse).astype(BF16)
                centre = jnp.sum(grad_t * parts_ref[0, b, k].astype(F32), axis=0, keepdims=True) * inverse
                slopes = raised * (dot(values, scaled_t) - centre).astype(BF16)
                results.append((dot(keys_t, slopes), dot(slopes, query), dot_nt(raised, scaled_t)))
            near, far = results
            for a in range(2):
                sums[a] = far[a + 1] if sums[a] is None else sums[a] + far[a + 1]
            outs = ((near[0] + far[0]).T * SCALE, near[1] * SCALE, near[2])
            for a, result in enumerate(outs):
                out_ref[:, a, :, at, :] = result.astype(BF16).reshape(count, frames, BLOCK, HEAD_DIM)
        sums[0] = sums[0] * SCALE
        for a in range(2):
            even_out[:, a] = sums[a][:half].reshape(count // 2, tokens, HEAD_DIM)
            odd_out[:, a] = sums[a][half:].reshape(count // 2, tokens, HEAD_DIM)

    all_rows = count * frames * part
    video_spec = pl.BlockSpec((count, 3, frames, part, HEAD_DIM), lambda h: (0, 0, 0, 0, h))
    ref_specs = [pl.BlockSpec((count // 2, 2, tokens, HEAD_DIM), lambda h: (0, 0, 0, h))] * 2
    out_ref_specs = [pl.BlockSpec((count // 2, 2, tokens, HEAD_DIM), lambda h: (0, 0, 0, h))] * 2
    return pl.pallas_call(
        kernel,
        grid=(heads,),
        in_specs=[video_spec, *ref_specs]
        + [by_head(array.shape[1:]) for array in saved]
        + [pl.BlockSpec((count, frames, part, HEAD_DIM), lambda h: (0, 0, 0, h))]
        + [ANY] * len(deps),
        out_specs=[video_spec, *out_ref_specs],
        out_shape=[jax.ShapeDtypeStruct(video.shape, BF16)]
        + [jax.ShapeDtypeStruct((*even.shape[:3], channels), F32)] * 2,
        compiler_params=LIMIT,
        cost_estimate=lasting(10),
    )(video, even, odd, *saved, grad, *deps)


def mix_back(cot, taps):
    full, held, channels = cot.shape
    reach = taps.shape[0]

    def kernel(taps_ref, cot_ref, out_ref):
        line = [cot_ref[f].astype(F32) for f in range(full)]
        for f in range(full):
            total = taps_ref[0:1, :] * line[f]
            for k in range(1, min(reach, full - f)):
                total = total + taps_ref[k : k + 1, :] * line[f + k]
            out_ref[f] = total.astype(BF16)

    block = pl.BlockSpec((full, held, HEAD_DIM), lambda h: (0, 0, h))
    return pl.pallas_call(
        kernel,
        grid=(channels // HEAD_DIM,),
        in_specs=[pl.BlockSpec((reach, HEAD_DIM), lambda h: (0, h)), block],
        out_specs=block,
        out_shape=jax.ShapeDtypeStruct(cot.shape, BF16),
        compiler_params=LIMIT,
        cost_estimate=lasting(1.5),
    )(taps, cot)


def mix(mixed, cot, taps, count, deps=()):
    full, part, channels = cot.shape
    reach = taps.shape[0]
    frames = full // count
    extra = -(-2 * reach // 16) * 16

    def kernel(taps_ref, mixed_ref, cot_ref, *rest):
        out_ref = rest[-1]
        line = []
        sums = [jnp.zeros((part, HEAD_DIM), F32) for _ in range(reach)]
        for f in range(full):
            line.append(mixed_ref[f].astype(F32))
            cot_line = cot_ref[f].astype(F32)
            total = jnp.zeros((part, HEAD_DIM), F32)
            for k in range(min(reach, f + 1)):
                total = total + taps_ref[k : k + 1, :] * line[f - k]
                sums[k] = sums[k] + cot_line * line[f - k]
            d, u = f // frames, f % frames
            out_ref[d, u * part : (u + 1) * part] = total.astype(BF16)
        sums = jnp.concatenate([jnp.sum(s, axis=0, keepdims=True) for s in sums], axis=0)
        high = sums.astype(BF16).astype(F32)
        zeros = jnp.zeros((extra - 2 * reach, HEAD_DIM), F32)
        rows = jnp.concatenate([high, sums - high, zeros], axis=0).astype(BF16)
        for d in range(count):
            out_ref[d, frames * part :] = rows

    block = pl.BlockSpec((full, part, HEAD_DIM), lambda h: (0, 0, h))
    return pl.pallas_call(
        kernel,
        grid=(channels // HEAD_DIM,),
        in_specs=[pl.BlockSpec((reach, HEAD_DIM), lambda h: (0, h)), block, block] + [ANY] * len(deps),
        out_specs=pl.BlockSpec((count, frames * part + extra, HEAD_DIM), lambda h: (0, 0, h)),
        out_shape=jax.ShapeDtypeStruct((count, frames * part + extra, channels), BF16),
        compiler_params=LIMIT,
        cost_estimate=lasting(3),
    )(taps, mixed, cot, *deps)


def project(attended, weight, deps=()):
    rows, channels = attended.shape
    depth = lax.axis_size("head")

    def kernel(attended_ref, weight_ref, *rest):
        for start in range(0, rows, ROW_TILE):
            at = slice(start, start + ROW_TILE)
            rest[-1][0, at] = dot(attended_ref[at], weight_ref[...]).astype(BF16)

    return pl.pallas_call(
        kernel,
        grid=(depth,),
        in_specs=[
            pl.BlockSpec((rows, channels), lambda j: (0, 0)),
            pl.BlockSpec((channels, channels), lambda j: (0, j)),
        ]
        + [ANY] * len(deps),
        out_specs=pl.BlockSpec((1, rows, channels), lambda j: (j, 0, 0)),
        out_shape=jax.ShapeDtypeStruct((depth, rows, channels), BF16),
        compiler_params=LIMIT,
        cost_estimate=lasting(4),
    )(attended, weight, *deps)


def project_back(blocks, weight, deps=()):
    depth, rows, channels = blocks.shape

    def kernel(blocks_ref, weight_ref, *rest):
        out_ref, total = rest[-2:]
        j = pl.program_id(0)
        for start in range(0, rows, ROW_TILE):
            at = slice(start, start + ROW_TILE)
            term = dot_nt(blocks_ref[0, at], weight_ref[...])

            @pl.when(j == 0)
            def _():
                total[at] = term

            @pl.when((j > 0) & (j < depth - 1))
            def _():
                total[at] += term

            @pl.when(j == depth - 1)
            def _():
                out_ref[at] = (total[at] + term).astype(BF16)

    return pl.pallas_call(
        kernel,
        grid=(depth,),
        in_specs=[
            pl.BlockSpec((1, rows, channels), lambda j: (j, 0, 0)),
            pl.BlockSpec((channels, channels), lambda j: (0, j)),
        ]
        + [ANY] * len(deps),
        out_specs=pl.BlockSpec((rows, channels), lambda j: (0, 0)),
        out_shape=jax.ShapeDtypeStruct((rows, channels), BF16),
        scratch_shapes=[pltpu.VMEM((rows, channels), F32)],
        compiler_params=LIMIT,
        cost_estimate=lasting(6),
    )(blocks, weight, *deps)


def weight_terms(attended, blocks, count, deps=()):
    chunks = len(attended)
    depth, rows, channels = blocks[0].shape
    parts = count // depth
    columns = channels // parts

    def kernel(*refs):
        out_ref, turned = refs[-2:]

        @pl.when(pl.program_id(0) == 0)
        def _():
            for c in range(chunks):
                turned[c] = refs[c][...].T

        total = None
        for c in range(chunks):
            term = dot(turned[c], refs[chunks + c][0])
            total = term if total is None else total + term
        for p in range(parts):
            out_ref[0, p] = total[:, p * columns : (p + 1) * columns].astype(BF16)

    return pl.pallas_call(
        kernel,
        grid=(depth,),
        in_specs=[pl.BlockSpec((rows, channels), lambda j: (0, 0))] * chunks
        + [pl.BlockSpec((1, rows, channels), lambda j: (j, 0, 0))] * chunks
        + [ANY] * len(deps),
        out_specs=pl.BlockSpec((1, parts, channels, columns), lambda j: (j, 0, 0, 0)),
        out_shape=jax.ShapeDtypeStruct((depth, parts, channels, columns), BF16),
        scratch_shapes=[pltpu.VMEM((chunks, channels, rows), BF16)],
        compiler_params=LIMIT,
        cost_estimate=lasting(7),
    )(*attended, *blocks, *deps)


def core_sums(terms, near, core, deps=()):
    chips, _, channels, columns = terms.shape

    def kernel(core_ref, terms_ref, near_ref, *rest):
        rest[-1][...] = (terms_ref[:, 0].astype(F32) + near_ref[...].astype(F32)).astype(BF16)

    block = pl.BlockSpec((1, channels, columns), lambda i, core: (i, 0, 0))
    return pl.pallas_call(
        kernel,
        grid_spec=pltpu.PrefetchScalarGridSpec(
            num_scalar_prefetch=1,
            grid=(chips,),
            in_specs=[pl.BlockSpec((1, 1, channels, columns), lambda i, core: (i, core[0], 0, 0)), block]
            + [ANY] * len(deps),
            out_specs=block,
        ),
        out_shape=jax.ShapeDtypeStruct((chips, channels, columns), BF16),
        compiler_params=LIMIT,
        cost_estimate=lasting(2.6),
    )(core.reshape(1).astype(jnp.int32), terms, near, *deps)


def per_device(
    queries,
    keys,
    values,
    ref_keys,
    ref_values,
    rate_scale,
    rate_reach,
    window_start,
    out_weight,
    conv_taps,
    cotangent,
):
    frames, spatial, channels = queries.shape
    count, depth = lax.axis_size("frame"), lax.axis_size("head")
    place = lax.axis_index("frame")
    part = spatial // count // CHUNKS
    rows = count * frames * part
    reach = conv_taps.shape[0]
    line = (count * frames, part, channels)

    cot, own, blocks = [], [], []
    for c in range(CHUNKS):
        packed = to_positions([cotangent], c, count)
        cot.append(travel(packed if c == 0 else after(packed, own[-1])).reshape(line))
        own.append(mix_back(cot[c], conv_taps))
        blocks.append(lax.all_gather(own[c].reshape(rows, channels), "head", axis=0))

    even, odd = collect(after(jnp.stack([ref_keys, ref_values]), own[0]), count, [own[-1]])
    bias = temporal_bias(rate_scale, rate_reach, window_start)

    video, before = [], even
    for c in range(CHUNKS):
        packed = to_positions([queries, keys, values], c, count)
        video.append(travel(after(packed, before)))
        before = video[-1]

    last = []
    attended, saved, mixed, back, finals = [], [], [], [], []

    def forward(c):
        nonlocal last
        out, *kept = attend(video[c], even, odd, bias, last)
        attended.append(out.reshape(rows, channels))
        saved.append(kept)
        shares = project(attended[c], out_weight)
        mixed.append(lax.psum_scatter(shares, "head", scatter_dimension=0, tiled=False))
        last = [shares]

    def pull(c):
        nonlocal last
        grad = project_back(blocks[c], out_weight, last)
        last = [grad]
        return grad.reshape(count, frames, part, channels)

    def backward(c, grad):
        nonlocal last
        results = attend_back(video[c], even, odd, saved[c], grad, last)
        last = [results[1]]
        back.append((travel(results[0]), results[1], results[2]))

    def finish(c):
        nonlocal last
        final = mix(mixed[c].reshape(line), cot[c], conv_taps, count, last)
        last = [final]
        return final

    forward(0)
    backward(0, pull(0))
    for c in range(1, CHUNKS):
        forward(c)

    last = [*last, back[0][0]]
    terms = weight_terms(attended, blocks, count, last)
    last = [terms]
    by_chip = terms.reshape(count // 2, 2, channels, terms.shape[3])
    core = place % 2
    near = swap(lax.dynamic_index_in_dim(by_chip, 1 - core, 1, keepdims=False), 1)
    grads = [pull(c) for c in range(1, CHUNKS)]
    sums = core_sums(by_chip, near, core, last)
    last = [sums]
    groups = [list(range(k, count, 2)) for k in range(2)]
    far = lax.all_to_all(sums, "frame", split_axis=0, concat_axis=0, axis_index_groups=groups, tiled=True)
    for c in range(1, CHUNKS):
        backward(c, grads[c - 1])

    last = [*last, far]
    for c in range(CHUNKS):
        finals.append(travel(finish(c)))
        last = [*last, back[c][0]] if c == 0 else last
    ref_even, ref_odd = (sum(b[k] for b in back) for k in (1, 2))
    ref_grads = reduce_pieces(ref_even, ref_odd, last)
    grad_weight = jnp.sum(far.astype(F32), axis=0)

    grads = [to_frames([b[0][:, a] for b in back]) for a in range(3)]
    held_rows = frames * part
    out = to_frames([f[:, :held_rows].reshape(count, frames, part, channels) for f in finals])
    taps_parts = jnp.sum(sum(f[:, held_rows : held_rows + 2 * reach].astype(F32) for f in finals), axis=0)
    taps_sum = taps_parts[:reach] + taps_parts[reach:]
    return (out, *grads, ref_grads[0], ref_grads[1], grad_weight, taps_sum)


def solution(mesh):
    video = P("frame", None, "head")
    tokens = P("frame", "head")
    return jax.shard_map(
        per_device,
        mesh=mesh,
        in_specs=(
            video,
            video,
            video,
            tokens,
            tokens,
            P("head"),
            P("head"),
            P(),
            P("head", None),
            P(None, "head"),
            video,
        ),
        out_specs=(video, video, video, video, tokens, tokens, P("head", "frame"), P(None, "head")),
        check_vma=False,
    )
```

```python
import jax
import jax.numpy as jnp
from jax import lax
from jax.experimental import pallas as pl
from jax.experimental.pallas import tpu as pltpu
from jax.sharding import PartitionSpec as P

HEAD_DIM = 128
SCALE = HEAD_DIM ** (-0.5)
LOG2E = 1.4426950408889634
BLOCK = 16
HIDDEN = -1e30
ROW_TILE = 256
VMEM = 24
COST = 1.15e9
CHUNKS = 2
BF16 = jnp.bfloat16
F32 = jnp.float32
ANY = pl.BlockSpec(memory_space=pl.ANY)
SMEM = pl.BlockSpec(memory_space=pltpu.SMEM)
LIMIT = pltpu.CompilerParams(vmem_limit_bytes=VMEM * 2**20)
BIG = pltpu.CompilerParams(vmem_limit_bytes=60 * 2**20)


def lasting(us):
    return pl.CostEstimate(flops=int(us * COST), bytes_accessed=0, transcendentals=0)


def dot(a, b):
    return lax.dot_general(a, b, (((1,), (0,)), ((), ())), preferred_element_type=F32)


def dot_nt(a, b):
    return lax.dot_general(a, b, (((1,), (1,)), ((), ())), preferred_element_type=F32)


def dot_tn(a, b):
    return lax.dot_general(a, b, (((0,), (0,)), ((), ())), preferred_element_type=F32)


def swap(value, s):
    count = lax.axis_size("frame")
    return lax.ppermute(value, "frame", [(i, i ^ s) for i in range(count)])


def collect(own, count, deps):
    pieces = [own] + [swap(own, s) for s in range(2, count, 2)]

    def kernel(*refs):
        for t in range(len(pieces)):
            refs[-1][t] = refs[t][...]

    even = pl.pallas_call(
        kernel,
        in_specs=[pl.BlockSpec(memory_space=pltpu.VMEM)] * len(pieces) + [ANY] * len(deps),
        out_specs=pl.BlockSpec(memory_space=pltpu.VMEM),
        out_shape=jax.ShapeDtypeStruct((len(pieces), *own.shape), own.dtype),
        compiler_params=LIMIT,
        cost_estimate=lasting(1.2),
    )(*pieces, *deps)
    return even, swap(even, 1)


def reduce_pieces(even, odd, deps):
    sums = after(even, *deps) + swap(odd.astype(BF16), 1).astype(F32)
    total = sums[0]
    for t in range(1, even.shape[0]):
        total = total + swap(sums[t].astype(BF16), 2 * t).astype(F32)
    return total


def to_positions(arrays, chunk, count):
    frames, spatial, channels = arrays[0].shape
    size = spatial // CHUNKS
    split = [
        lax.slice_in_dim(a, chunk * size, (chunk + 1) * size, axis=1)
        .reshape(frames, count, 1, size // count, channels)
        .transpose(1, 2, 0, 3, 4)
        for a in arrays
    ]
    return jnp.concatenate(split, axis=1)


def after(value, *others):
    return lax.optimization_barrier((value, *others))[0]


def travel(value):
    return lax.all_to_all(value, "frame", split_axis=0, concat_axis=0, tiled=True)


def to_frames(values):
    count, frames, part, channels = values[0].shape
    return jnp.concatenate(
        [v.transpose(1, 0, 2, 3).reshape(frames, count * part, channels) for v in values], axis=1
    )


def temporal_bias(rate_scale, rate_reach, starts):
    places = jnp.arange(starts.shape[0], dtype=jnp.int32)
    distance = jnp.abs(places[:, None] - places[None, :]).astype(F32)
    penalty = -rate_scale[:, None, None] * jnp.log1p(rate_reach[:, None, None] * distance[None])
    allowed = (places[:, None] <= places[None, :]) & (places[:, None] >= starts[None, :])
    return jnp.repeat(jnp.where(allowed[None], penalty * LOG2E, HIDDEN), BLOCK, axis=2)


def widen(bias):
    frames, rows = bias.shape
    wide = jnp.broadcast_to(bias[:, None, :], (frames, BLOCK, rows)).reshape(rows, rows)
    key_place = lax.broadcasted_iota(jnp.int32, (rows, rows), 0) % BLOCK
    query_place = lax.broadcasted_iota(jnp.int32, (rows, rows), 1) % BLOCK
    return jnp.where(key_place == query_place, wide, HIDDEN)


def weights_of(scores):
    raised = jnp.exp2(scores - jnp.max(scores, axis=0, keepdims=True))
    return raised, 1.0 / jnp.sum(raised, axis=0, keepdims=True)


def stacked(ref, index):
    value = ref[:, index]
    return value.reshape(value.shape[0] * value.shape[1], HEAD_DIM)


def attend(video, even, odd, bias, deps=()):
    count, _, frames, part, channels = video.shape
    tokens = even.shape[2]
    heads = channels // HEAD_DIM
    rows = count * frames * BLOCK
    number = part // BLOCK
    all_tokens = tokens * count

    def kernel(video_ref, even_ref, odd_ref, bias_ref, *rest):
        out_ref, near_ref, far_ref, inverse_ref, parts_ref = rest[-5:]
        ref_key = jnp.concatenate([stacked(even_ref, 0), stacked(odd_ref, 0)], axis=0)
        ref_value_t = jnp.concatenate([stacked(even_ref, 1), stacked(odd_ref, 1)], axis=0).T
        wide = widen(bias_ref[0])
        for b in range(number):
            at = slice(b * BLOCK, (b + 1) * BLOCK)
            query, key, value = (video_ref[:, a, :, at, :].reshape(rows, HEAD_DIM) for a in range(3))
            total = None
            for k, (scores, value_t, keep) in enumerate(
                (
                    (dot_nt(key, query) * (SCALE * LOG2E) + wide, value.T, near_ref),
                    (dot_nt(ref_key, query) * (SCALE * LOG2E), ref_value_t, far_ref),
                )
            ):
                raised, inverse = weights_of(scores)
                raised = raised.astype(BF16)
                keep[0, b] = raised
                inverse_ref[0, b, k : k + 1, :] = inverse
                term = dot(value_t, raised) * inverse
                parts_ref[0, b, k] = term.astype(BF16)
                total = term if total is None else total + term
            out_ref[:, :, at, :] = total.T.astype(BF16).reshape(count, frames, BLOCK, HEAD_DIM)

    all_rows = count * frames * part
    saved = [
        ((number, rows, rows), BF16),
        ((number, all_tokens, rows), BF16),
        ((number, 2, rows), F32),
        ((number, 2, HEAD_DIM, rows), BF16),
    ]
    return pl.pallas_call(
        kernel,
        grid=(heads,),
        in_specs=[pl.BlockSpec((count, 3, frames, part, HEAD_DIM), lambda h: (0, 0, 0, 0, h))]
        + [pl.BlockSpec((count // 2, 2, tokens, HEAD_DIM), lambda h: (0, 0, 0, h))] * 2
        + [pl.BlockSpec((1, count * frames, rows), lambda h: (h, 0, 0))]
        + [ANY] * len(deps),
        out_specs=[pl.BlockSpec((count, frames, part, HEAD_DIM), lambda h: (0, 0, 0, h))]
        + [by_head(shape) for shape, _ in saved],
        out_shape=[jax.ShapeDtypeStruct((count, frames, part, channels), BF16)]
        + [jax.ShapeDtypeStruct((heads, *shape), kind) for shape, kind in saved],
        compiler_params=BIG,
        cost_estimate=lasting(8),
    )(video, even, odd, bias, *deps)


def by_head(shape):
    return pl.BlockSpec((1, *shape), lambda h: (h,) + (0,) * len(shape))


def attend_back(video, even, odd, saved, grad, arrays, deps=()):
    count, _, frames, part, channels = video.shape
    tokens = even.shape[2]
    heads = channels // HEAD_DIM
    rows = count * frames * BLOCK
    half = tokens * count // 2

    def kernel(video_ref, even_ref, odd_ref, near_ref, far_ref, inverse_ref, parts_ref, grad_ref, *rest):
        out_ref, even_out, odd_out = rest[-3:]
        ref_key = jnp.concatenate([stacked(even_ref, 0), stacked(odd_ref, 0)], axis=0)
        ref_value = jnp.concatenate([stacked(even_ref, 1), stacked(odd_ref, 1)], axis=0)
        ref_key_t = ref_key.T
        sums = [None, None]
        for b in range(part // BLOCK):
            at = slice(b * BLOCK, (b + 1) * BLOCK)
            query, key, value = (video_ref[:, a, :, at, :].reshape(rows, HEAD_DIM) for a in range(3))
            grad_t = grad_ref[:, :, at, :].reshape(rows, HEAD_DIM).T.astype(F32)
            results = []
            for k, (raised, keys_t, values) in enumerate(
                ((near_ref[0, b], key.T, value), (far_ref[0, b], ref_key_t, ref_value))
            ):
                inverse = inverse_ref[0, b, k : k + 1, :]
                scaled_t = (grad_t * inverse).astype(BF16)
                centre = jnp.sum(grad_t * parts_ref[0, b, k].astype(F32), axis=0, keepdims=True) * inverse
                slopes = raised * (dot(values, scaled_t) - centre).astype(BF16)
                results.append((dot(keys_t, slopes), dot(slopes, query), dot_nt(raised, scaled_t)))
            near, far = results
            for a in range(2):
                sums[a] = far[a + 1] if sums[a] is None else sums[a] + far[a + 1]
            outs = ((near[0] + far[0]).T * SCALE, near[1] * SCALE, near[2])
            for a, result in enumerate(outs):
                out_ref[:, a, :, at, :] = result.astype(BF16).reshape(count, frames, BLOCK, HEAD_DIM)
        sums[0] = sums[0] * SCALE
        for a in range(2):
            even_out[:, a] = sums[a][:half].reshape(count // 2, tokens, HEAD_DIM)
            odd_out[:, a] = sums[a][half:].reshape(count // 2, tokens, HEAD_DIM)

    all_rows = count * frames * part
    video_spec = pl.BlockSpec((count, 3, frames, part, HEAD_DIM), lambda h: (0, 0, 0, 0, h))
    ref_specs = [pl.BlockSpec((count // 2, 2, tokens, HEAD_DIM), lambda h: (0, 0, 0, h))] * 2
    out_ref_specs = [pl.BlockSpec((count // 2, 2, tokens, HEAD_DIM), lambda h: (0, 0, 0, h))] * 2
    return pl.pallas_call(
        kernel,
        grid=(heads,),
        in_specs=[video_spec, *ref_specs]
        + [by_head(array.shape[1:]) for array in saved]
        + [pl.BlockSpec((count, frames, part, HEAD_DIM), lambda h: (0, 0, 0, h))]
        + [ANY] * len(deps),
        out_specs=[video_spec, *out_ref_specs],
        out_shape=[jax.ShapeDtypeStruct((count, arrays, frames, part, channels), BF16)]
        + [jax.ShapeDtypeStruct((*even.shape[:3], channels), F32)] * 2,
        compiler_params=BIG,
        cost_estimate=lasting(10),
    )(video, even, odd, *saved, grad, *deps)


def mix_back(cot, taps):
    full, held, channels = cot.shape
    reach = taps.shape[0]

    def kernel(taps_ref, cot_ref, out_ref):
        line = [cot_ref[f].astype(F32) for f in range(full)]
        for f in range(full):
            total = taps_ref[0:1, :] * line[f]
            for k in range(1, min(reach, full - f)):
                total = total + taps_ref[k : k + 1, :] * line[f + k]
            out_ref[f] = total.astype(BF16)

    block = pl.BlockSpec((full, held, HEAD_DIM), lambda h: (0, 0, h))
    return pl.pallas_call(
        kernel,
        grid=(channels // HEAD_DIM,),
        in_specs=[pl.BlockSpec((reach, HEAD_DIM), lambda h: (0, h)), block],
        out_specs=block,
        out_shape=jax.ShapeDtypeStruct(cot.shape, BF16),
        compiler_params=LIMIT,
        cost_estimate=lasting(1.5),
    )(taps, cot)


def mix(mixed, cot, taps, count, room=None, taps_before=None, deps=()):
    full, part, channels = cot.shape
    reach = taps.shape[0]
    frames = full // count
    last = taps_before is not None
    extra = -(-2 * reach // 16) * 16

    def kernel(taps_ref, mixed_ref, cot_ref, *rest):
        line = []
        sums = [jnp.zeros((part, HEAD_DIM), F32) for _ in range(reach)]
        for f in range(full):
            line.append(mixed_ref[f].astype(F32))
            cot_line = cot_ref[f].astype(F32)
            total = jnp.zeros((part, HEAD_DIM), F32)
            for k in range(min(reach, f + 1)):
                total = total + taps_ref[k : k + 1, :] * line[f - k]
                sums[k] = sums[k] + cot_line * line[f - k]
            d, u = f // frames, f % frames
            if last:
                rest[-1][d, u * part : (u + 1) * part] = total.astype(BF16)
            else:
                rest[-2][d, 0, u] = total.astype(BF16)
        sums = jnp.concatenate([jnp.sum(s, axis=0, keepdims=True) for s in sums], axis=0)
        if last:
            sums = sums + rest[0][...]
            high = sums.astype(BF16).astype(F32)
            zeros = jnp.zeros((extra - 2 * reach, HEAD_DIM), F32)
            rows = jnp.concatenate([high, sums - high, zeros], axis=0).astype(BF16)
            for d in range(count):
                rest[-1][d, frames * part :] = rows
        else:
            rest[-1][...] = sums

    block = pl.BlockSpec((full, part, HEAD_DIM), lambda h: (0, 0, h))
    taps_block = pl.BlockSpec((reach, HEAD_DIM), lambda h: (0, h))
    if last:
        out_specs = pl.BlockSpec((count, frames * part + extra, HEAD_DIM), lambda h: (0, 0, h))
        out_shape = jax.ShapeDtypeStruct((count, frames * part + extra, channels), BF16)
    else:
        slot = room.shape[1] - 1
        out_specs = [
            pl.BlockSpec((count, 1, frames, part, HEAD_DIM), lambda h: (0, slot, 0, 0, h)),
            taps_block,
        ]
        out_shape = [
            jax.ShapeDtypeStruct(room.shape, BF16),
            jax.ShapeDtypeStruct(taps.shape, F32),
        ]
    return pl.pallas_call(
        kernel,
        grid=(channels // HEAD_DIM,),
        in_specs=[taps_block, block, block, taps_block if last else ANY] + [ANY] * len(deps),
        input_output_aliases={} if last else {3: 0},
        out_specs=out_specs,
        out_shape=out_shape,
        compiler_params=LIMIT,
        cost_estimate=lasting(3),
    )(taps, mixed, cot, taps_before if last else room, *deps)


def project(attended, weight, deps=()):
    rows, channels = attended.shape
    depth = lax.axis_size("head")

    def kernel(attended_ref, weight_ref, *rest):
        for start in range(0, rows, ROW_TILE):
            at = slice(start, start + ROW_TILE)
            rest[-1][0, at] = dot(attended_ref[at], weight_ref[...]).astype(BF16)

    return pl.pallas_call(
        kernel,
        grid=(depth,),
        in_specs=[
            pl.BlockSpec((rows, channels), lambda j: (0, 0)),
            pl.BlockSpec((channels, channels), lambda j: (0, j)),
        ]
        + [ANY] * len(deps),
        out_specs=pl.BlockSpec((1, rows, channels), lambda j: (j, 0, 0)),
        out_shape=jax.ShapeDtypeStruct((depth, rows, channels), BF16),
        compiler_params=BIG,
        cost_estimate=lasting(4),
    )(attended, weight, *deps)


def project_back(blocks, weight, deps=()):
    depth, rows, channels = blocks.shape

    def kernel(blocks_ref, weight_ref, *rest):
        out_ref, total = rest[-2:]
        j = pl.program_id(0)
        for start in range(0, rows, ROW_TILE):
            at = slice(start, start + ROW_TILE)
            term = dot_nt(blocks_ref[0, at], weight_ref[...])

            @pl.when(j == 0)
            def _():
                total[at] = term

            @pl.when((j > 0) & (j < depth - 1))
            def _():
                total[at] += term

            @pl.when(j == depth - 1)
            def _():
                out_ref[at] = (total[at] + term).astype(BF16)

    return pl.pallas_call(
        kernel,
        grid=(depth,),
        in_specs=[
            pl.BlockSpec((1, rows, channels), lambda j: (j, 0, 0)),
            pl.BlockSpec((channels, channels), lambda j: (0, j)),
        ]
        + [ANY] * len(deps),
        out_specs=pl.BlockSpec((rows, channels), lambda j: (0, 0)),
        out_shape=jax.ShapeDtypeStruct((rows, channels), BF16),
        scratch_shapes=[pltpu.VMEM((rows, channels), F32)],
        compiler_params=BIG,
        cost_estimate=lasting(6),
    )(blocks, weight, *deps)


def weight_terms(attended, blocks, count, deps=()):
    chunks = len(attended)
    depth, rows, channels = blocks[0].shape
    parts = count // depth
    columns = channels // parts

    def kernel(*refs):
        out_ref, turned = refs[-2:]

        @pl.when(pl.program_id(0) == 0)
        def _():
            for c in range(chunks):
                turned[c] = refs[c][...].T

        total = None
        for c in range(chunks):
            term = dot(turned[c], refs[chunks + c][0])
            total = term if total is None else total + term
        for p in range(parts):
            out_ref[0, p] = total[:, p * columns : (p + 1) * columns].astype(BF16)

    return pl.pallas_call(
        kernel,
        grid=(depth,),
        in_specs=[pl.BlockSpec((rows, channels), lambda j: (0, 0))] * chunks
        + [pl.BlockSpec((1, rows, channels), lambda j: (j, 0, 0))] * chunks
        + [ANY] * len(deps),
        out_specs=pl.BlockSpec((1, parts, channels, columns), lambda j: (j, 0, 0, 0)),
        out_shape=jax.ShapeDtypeStruct((depth, parts, channels, columns), BF16),
        scratch_shapes=[pltpu.VMEM((chunks, channels, rows), BF16)],
        compiler_params=BIG,
        cost_estimate=lasting(7),
    )(*attended, *blocks, *deps)


def core_sums(terms, near, core, deps=()):
    chips, _, channels, columns = terms.shape

    def kernel(core_ref, terms_ref, near_ref, *rest):
        rest[-1][...] = (terms_ref[:, 0].astype(F32) + near_ref[...].astype(F32)).astype(BF16)

    block = pl.BlockSpec((1, channels, columns), lambda i, core: (i, 0, 0))
    return pl.pallas_call(
        kernel,
        grid_spec=pltpu.PrefetchScalarGridSpec(
            num_scalar_prefetch=1,
            grid=(chips,),
            in_specs=[pl.BlockSpec((1, 1, channels, columns), lambda i, core: (i, core[0], 0, 0)), block]
            + [ANY] * len(deps),
            out_specs=block,
        ),
        out_shape=jax.ShapeDtypeStruct((chips, channels, columns), BF16),
        compiler_params=LIMIT,
        cost_estimate=lasting(2.6),
    )(core.reshape(1).astype(jnp.int32), terms, near, *deps)


def per_device(
    queries,
    keys,
    values,
    ref_keys,
    ref_values,
    rate_scale,
    rate_reach,
    window_start,
    out_weight,
    conv_taps,
    cotangent,
):
    frames, spatial, channels = queries.shape
    count, depth = lax.axis_size("frame"), lax.axis_size("head")
    place = lax.axis_index("frame")
    part = spatial // count // CHUNKS
    rows = count * frames * part
    reach = conv_taps.shape[0]
    line = (count * frames, part, channels)

    cot, own, blocks = [], [], []
    for c in range(CHUNKS):
        packed = to_positions([cotangent], c, count)
        cot.append(travel(packed if c == 0 else after(packed, own[-1])).reshape(line))
        own.append(mix_back(cot[c], conv_taps))
        blocks.append(lax.all_gather(own[c].reshape(rows, channels), "head", axis=0))

    even, odd = collect(after(jnp.stack([ref_keys, ref_values]), own[0]), count, [own[-1]])
    bias = temporal_bias(rate_scale, rate_reach, window_start)

    video, before = [], even
    for c in range(CHUNKS):
        packed = to_positions([queries, keys, values], c, count)
        video.append(travel(after(packed, before)))
        before = video[-1]

    last = []
    attended, saved, mixed = [], [], []

    def forward(c):
        nonlocal last
        out, *kept = attend(video[c], even, odd, bias, last)
        attended.append(out.reshape(rows, channels))
        saved.append(kept)
        shares = project(attended[c], out_weight)
        mixed.append(lax.psum_scatter(shares, "head", scatter_dimension=0, tiled=False))
        last = [shares]

    def pull(c):
        nonlocal last
        grad = project_back(blocks[c], out_weight, last)
        last = [grad]
        return grad.reshape(count, frames, part, channels)

    def backward(c, grad, arrays):
        nonlocal last
        results = attend_back(video[c], even, odd, saved[c], grad, arrays, last)
        last = [results[1]]
        return results

    forward(0)
    first_back, even_first, odd_first = backward(0, pull(0), 3)
    first_back = travel(first_back)
    forward(1)

    terms = weight_terms(attended, blocks, count, [*last, first_back])
    by_chip = terms.reshape(count // 2, 2, channels, terms.shape[3])
    core = place % 2
    near = swap(lax.dynamic_index_in_dim(by_chip, 1 - core, 1, keepdims=False), 1)
    sums = core_sums(by_chip, near, core)
    last = [sums]
    groups = [list(range(k, count, 2)) for k in range(2)]
    far = lax.all_to_all(sums, "frame", split_axis=0, concat_axis=0, axis_index_groups=groups, tiled=True)

    second_back, even_second, odd_second = backward(1, pull(1), 4)
    second_back, taps_first = mix(
        mixed[0].reshape(line), cot[0], conv_taps, count, room=second_back, deps=[*last, far]
    )
    second_back = travel(second_back)
    ref_grads = reduce_pieces(even_first + even_second, odd_first + odd_second, [second_back])
    final = mix(mixed[1].reshape(line), cot[1], conv_taps, count, taps_before=taps_first, deps=[ref_grads])
    final = travel(final)
    grad_weight = jnp.sum(far.astype(F32), axis=0)

    grads = [to_frames([first_back[:, a], second_back[:, a]]) for a in range(3)]
    held_rows = frames * part
    out = to_frames([second_back[:, 3], final[:, :held_rows].reshape(count, frames, part, channels)])
    taps_parts = jnp.sum(final[:, held_rows : held_rows + 2 * reach].astype(F32), axis=0)
    taps_sum = taps_parts[:reach] + taps_parts[reach:]
    return (out, *grads, ref_grads[0], ref_grads[1], grad_weight, taps_sum)


def solution(mesh):
    video = P("frame", None, "head")
    tokens = P("frame", "head")
    return jax.shard_map(
        per_device,
        mesh=mesh,
        in_specs=(
            video,
            video,
            video,
            tokens,
            tokens,
            P("head"),
            P("head"),
            P(),
            P("head", None),
            P(None, "head"),
            video,
        ),
        out_specs=(video, video, video, video, tokens, tokens, P("head", "frame"), P(None, "head")),
        check_vma=False,
    )
```

```python
import jax
import jax.numpy as jnp
from jax import lax
from jax.experimental import pallas as pl
from jax.experimental.pallas import tpu as pltpu
from jax.sharding import PartitionSpec as P

HEAD_DIM = 128
SCALE = HEAD_DIM ** (-0.5)
LOG2E = 1.4426950408889634
BLOCK = 16
HIDDEN = -1e30
ROW_TILE = 256
VMEM = 24
COST = 2.3e+09
CHUNKS = 2
BF16 = jnp.bfloat16
F32 = jnp.float32
ANY = pl.BlockSpec(memory_space=pl.ANY)
SMEM = pl.BlockSpec(memory_space=pltpu.SMEM)
LIMIT = pltpu.CompilerParams(vmem_limit_bytes=VMEM * 2**20)
BIG = pltpu.CompilerParams(vmem_limit_bytes=60 * 2**20)


def lasting(us):
    return pl.CostEstimate(flops=int(us * COST), bytes_accessed=0, transcendentals=0)


def dot(a, b):
    return lax.dot_general(a, b, (((1,), (0,)), ((), ())), preferred_element_type=F32)


def dot_nt(a, b):
    return lax.dot_general(a, b, (((1,), (1,)), ((), ())), preferred_element_type=F32)


def dot_tn(a, b):
    return lax.dot_general(a, b, (((0,), (0,)), ((), ())), preferred_element_type=F32)


def swap(value, s):
    count = lax.axis_size("frame")
    return lax.ppermute(value, "frame", [(i, i ^ s) for i in range(count)])


def collect(own, count, deps):
    pieces = [own] + [swap(own, s) for s in range(2, count, 2)]

    def kernel(*refs):
        for t in range(len(pieces)):
            refs[-1][t] = refs[t][...]

    even = pl.pallas_call(
        kernel,
        in_specs=[pl.BlockSpec(memory_space=pltpu.VMEM)] * len(pieces) + [ANY] * len(deps),
        out_specs=pl.BlockSpec(memory_space=pltpu.VMEM),
        out_shape=jax.ShapeDtypeStruct((len(pieces), *own.shape), own.dtype),
        compiler_params=LIMIT,
        cost_estimate=lasting(1.2),
    )(*pieces, *deps)
    return even, swap(even, 1)


def reduce_pieces(even, odd, deps):
    sums = after(even, *deps) + swap(odd.astype(BF16), 1).astype(F32)
    total = sums[0]
    for t in range(1, even.shape[0]):
        total = total + swap(sums[t].astype(BF16), 2 * t).astype(F32)
    return total


def to_positions(arrays, chunk, count):
    frames, spatial, channels = arrays[0].shape
    size = spatial // CHUNKS
    split = [
        lax.slice_in_dim(a, chunk * size, (chunk + 1) * size, axis=1)
        .reshape(frames, count, 1, size // count, channels)
        .transpose(1, 2, 0, 3, 4)
        for a in arrays
    ]
    return jnp.concatenate(split, axis=1)


def after(value, *others):
    return lax.optimization_barrier((value, *others))[0]


def travel(value):
    return lax.all_to_all(value, "frame", split_axis=0, concat_axis=0, tiled=True)


def to_frames(values):
    count, frames, part, channels = values[0].shape
    return jnp.concatenate(
        [v.transpose(1, 0, 2, 3).reshape(frames, count * part, channels) for v in values], axis=1
    )


def temporal_bias(rate_scale, rate_reach, starts):
    places = jnp.arange(starts.shape[0], dtype=jnp.int32)
    distance = jnp.abs(places[:, None] - places[None, :]).astype(F32)
    penalty = -rate_scale[:, None, None] * jnp.log1p(rate_reach[:, None, None] * distance[None])
    allowed = (places[:, None] <= places[None, :]) & (places[:, None] >= starts[None, :])
    return jnp.repeat(jnp.where(allowed[None], penalty * LOG2E, HIDDEN), BLOCK, axis=2)


def widen(bias):
    frames, rows = bias.shape
    wide = jnp.broadcast_to(bias[:, None, :], (frames, BLOCK, rows)).reshape(rows, rows)
    key_place = lax.broadcasted_iota(jnp.int32, (rows, rows), 0) % BLOCK
    query_place = lax.broadcasted_iota(jnp.int32, (rows, rows), 1) % BLOCK
    return jnp.where(key_place == query_place, wide, HIDDEN)


def weights_of(scores):
    raised = jnp.exp2(scores - jnp.max(scores, axis=0, keepdims=True))
    return raised, 1.0 / jnp.sum(raised, axis=0, keepdims=True)


def stacked(ref, index):
    value = ref[:, index]
    return value.reshape(value.shape[0] * value.shape[1], HEAD_DIM)


def attend(video, even, odd, bias, deps=()):
    count, _, frames, part, channels = video.shape
    tokens = even.shape[2]
    heads = channels // HEAD_DIM
    rows = count * frames * BLOCK
    number = part // BLOCK
    all_tokens = tokens * count

    def kernel(video_ref, even_ref, odd_ref, bias_ref, *rest):
        out_ref, near_ref, far_ref, inverse_ref, parts_ref = rest[-5:]
        ref_key = jnp.concatenate([stacked(even_ref, 0), stacked(odd_ref, 0)], axis=0)
        ref_value_t = jnp.concatenate([stacked(even_ref, 1), stacked(odd_ref, 1)], axis=0).T
        wide = widen(bias_ref[0])
        for b in range(number):
            at = slice(b * BLOCK, (b + 1) * BLOCK)
            query, key, value = (video_ref[:, a, :, at, :].reshape(rows, HEAD_DIM) for a in range(3))
            total = None
            for k, (scores, value_t, keep) in enumerate(
                (
                    (dot_nt(key, query) * (SCALE * LOG2E) + wide, value.T, near_ref),
                    (dot_nt(ref_key, query) * (SCALE * LOG2E), ref_value_t, far_ref),
                )
            ):
                raised, inverse = weights_of(scores)
                raised = raised.astype(BF16)
                keep[0, b] = raised
                inverse_ref[0, b, k : k + 1, :] = inverse
                term = dot(value_t, raised) * inverse
                parts_ref[0, b, k] = term.astype(BF16)
                total = term if total is None else total + term
            out_ref[:, :, at, :] = total.T.astype(BF16).reshape(count, frames, BLOCK, HEAD_DIM)

    all_rows = count * frames * part
    saved = [
        ((number, rows, rows), BF16),
        ((number, all_tokens, rows), BF16),
        ((number, 2, rows), F32),
        ((number, 2, HEAD_DIM, rows), BF16),
    ]
    return pl.pallas_call(
        kernel,
        grid=(heads,),
        in_specs=[pl.BlockSpec((count, 3, frames, part, HEAD_DIM), lambda h: (0, 0, 0, 0, h))]
        + [pl.BlockSpec((count // 2, 2, tokens, HEAD_DIM), lambda h: (0, 0, 0, h))] * 2
        + [pl.BlockSpec((1, count * frames, rows), lambda h: (h, 0, 0))]
        + [ANY] * len(deps),
        out_specs=[pl.BlockSpec((count, frames, part, HEAD_DIM), lambda h: (0, 0, 0, h))]
        + [by_head(shape) for shape, _ in saved],
        out_shape=[jax.ShapeDtypeStruct((count, frames, part, channels), BF16)]
        + [jax.ShapeDtypeStruct((heads, *shape), kind) for shape, kind in saved],
        compiler_params=BIG,
        cost_estimate=lasting(8),
    )(video, even, odd, bias, *deps)


def by_head(shape):
    return pl.BlockSpec((1, *shape), lambda h: (h,) + (0,) * len(shape))


def attend_back(video, even, odd, saved, grad, arrays, deps=()):
    count, _, frames, part, channels = video.shape
    tokens = even.shape[2]
    heads = channels // HEAD_DIM
    rows = count * frames * BLOCK
    half = tokens * count // 2

    def kernel(video_ref, even_ref, odd_ref, near_ref, far_ref, inverse_ref, parts_ref, grad_ref, *rest):
        out_ref, even_out, odd_out = rest[-3:]
        ref_key = jnp.concatenate([stacked(even_ref, 0), stacked(odd_ref, 0)], axis=0)
        ref_value = jnp.concatenate([stacked(even_ref, 1), stacked(odd_ref, 1)], axis=0)
        ref_key_t = ref_key.T
        sums = [None, None]
        for b in range(part // BLOCK):
            at = slice(b * BLOCK, (b + 1) * BLOCK)
            query, key, value = (video_ref[:, a, :, at, :].reshape(rows, HEAD_DIM) for a in range(3))
            grad_t = grad_ref[:, :, at, :].reshape(rows, HEAD_DIM).T.astype(F32)
            results = []
            for k, (raised, keys_t, values) in enumerate(
                ((near_ref[0, b], key.T, value), (far_ref[0, b], ref_key_t, ref_value))
            ):
                inverse = inverse_ref[0, b, k : k + 1, :]
                scaled_t = (grad_t * inverse).astype(BF16)
                centre = jnp.sum(grad_t * parts_ref[0, b, k].astype(F32), axis=0, keepdims=True) * inverse
                slopes = raised * (dot(values, scaled_t) - centre).astype(BF16)
                results.append((dot(keys_t, slopes), dot(slopes, query), dot_nt(raised, scaled_t)))
            near, far = results
            for a in range(2):
                sums[a] = far[a + 1] if sums[a] is None else sums[a] + far[a + 1]
            outs = ((near[0] + far[0]).T * SCALE, near[1] * SCALE, near[2])
            for a, result in enumerate(outs):
                out_ref[:, a, :, at, :] = result.astype(BF16).reshape(count, frames, BLOCK, HEAD_DIM)
        sums[0] = sums[0] * SCALE
        for a in range(2):
            even_out[:, a] = sums[a][:half].reshape(count // 2, tokens, HEAD_DIM)
            odd_out[:, a] = sums[a][half:].reshape(count // 2, tokens, HEAD_DIM)

    all_rows = count * frames * part
    video_spec = pl.BlockSpec((count, 3, frames, part, HEAD_DIM), lambda h: (0, 0, 0, 0, h))
    ref_specs = [pl.BlockSpec((count // 2, 2, tokens, HEAD_DIM), lambda h: (0, 0, 0, h))] * 2
    out_ref_specs = [pl.BlockSpec((count // 2, 2, tokens, HEAD_DIM), lambda h: (0, 0, 0, h))] * 2
    return pl.pallas_call(
        kernel,
        grid=(heads,),
        in_specs=[video_spec, *ref_specs]
        + [by_head(array.shape[1:]) for array in saved]
        + [pl.BlockSpec((count, frames, part, HEAD_DIM), lambda h: (0, 0, 0, h))]
        + [ANY] * len(deps),
        out_specs=[video_spec, *out_ref_specs],
        out_shape=[jax.ShapeDtypeStruct((count, arrays, frames, part, channels), BF16)]
        + [jax.ShapeDtypeStruct((*even.shape[:3], channels), F32)] * 2,
        compiler_params=BIG,
        cost_estimate=lasting(10),
    )(video, even, odd, *saved, grad, *deps)


def mix_back(cot, taps):
    full, held, channels = cot.shape
    reach = taps.shape[0]

    def kernel(taps_ref, cot_ref, out_ref):
        line = [cot_ref[f].astype(F32) for f in range(full)]
        for f in range(full):
            total = taps_ref[0:1, :] * line[f]
            for k in range(1, min(reach, full - f)):
                total = total + taps_ref[k : k + 1, :] * line[f + k]
            out_ref[f] = total.astype(BF16)

    block = pl.BlockSpec((full, held, HEAD_DIM), lambda h: (0, 0, h))
    return pl.pallas_call(
        kernel,
        grid=(channels // HEAD_DIM,),
        in_specs=[pl.BlockSpec((reach, HEAD_DIM), lambda h: (0, h)), block],
        out_specs=block,
        out_shape=jax.ShapeDtypeStruct(cot.shape, BF16),
        compiler_params=LIMIT,
        cost_estimate=lasting(1.5),
    )(taps, cot)


def mix(mixed, cot, taps, count, room=None, taps_before=None, deps=()):
    full, part, channels = cot.shape
    reach = taps.shape[0]
    frames = full // count
    last = taps_before is not None
    extra = -(-2 * reach // 16) * 16

    def kernel(taps_ref, mixed_ref, cot_ref, *rest):
        line = []
        sums = [jnp.zeros((part, HEAD_DIM), F32) for _ in range(reach)]
        for f in range(full):
            line.append(mixed_ref[f].astype(F32))
            cot_line = cot_ref[f].astype(F32)
            total = jnp.zeros((part, HEAD_DIM), F32)
            for k in range(min(reach, f + 1)):
                total = total + taps_ref[k : k + 1, :] * line[f - k]
                sums[k] = sums[k] + cot_line * line[f - k]
            d, u = f // frames, f % frames
            if last:
                rest[-1][d, u * part : (u + 1) * part] = total.astype(BF16)
            else:
                rest[-2][d, 0, u] = total.astype(BF16)
        sums = jnp.concatenate([jnp.sum(s, axis=0, keepdims=True) for s in sums], axis=0)
        if last:
            sums = sums + rest[0][...]
            high = sums.astype(BF16).astype(F32)
            zeros = jnp.zeros((extra - 2 * reach, HEAD_DIM), F32)
            rows = jnp.concatenate([high, sums - high, zeros], axis=0).astype(BF16)
            for d in range(count):
                rest[-1][d, frames * part :] = rows
        else:
            rest[-1][...] = sums

    block = pl.BlockSpec((full, part, HEAD_DIM), lambda h: (0, 0, h))
    taps_block = pl.BlockSpec((reach, HEAD_DIM), lambda h: (0, h))
    if last:
        out_specs = pl.BlockSpec((count, frames * part + extra, HEAD_DIM), lambda h: (0, 0, h))
        out_shape = jax.ShapeDtypeStruct((count, frames * part + extra, channels), BF16)
    else:
        slot = room.shape[1] - 1
        out_specs = [
            pl.BlockSpec((count, 1, frames, part, HEAD_DIM), lambda h: (0, slot, 0, 0, h)),
            taps_block,
        ]
        out_shape = [
            jax.ShapeDtypeStruct(room.shape, BF16),
            jax.ShapeDtypeStruct(taps.shape, F32),
        ]
    return pl.pallas_call(
        kernel,
        grid=(channels // HEAD_DIM,),
        in_specs=[taps_block, block, block, taps_block if last else ANY] + [ANY] * len(deps),
        input_output_aliases={} if last else {3: 0},
        out_specs=out_specs,
        out_shape=out_shape,
        compiler_params=LIMIT,
        cost_estimate=lasting(3),
    )(taps, mixed, cot, taps_before if last else room, *deps)


def project(attended, weight, deps=()):
    rows, channels = attended.shape
    depth = lax.axis_size("head")

    def kernel(attended_ref, weight_ref, *rest):
        for start in range(0, rows, ROW_TILE):
            at = slice(start, start + ROW_TILE)
            rest[-1][0, at] = dot(attended_ref[at], weight_ref[...]).astype(BF16)

    return pl.pallas_call(
        kernel,
        grid=(depth,),
        in_specs=[
            pl.BlockSpec((rows, channels), lambda j: (0, 0)),
            pl.BlockSpec((channels, channels), lambda j: (0, j)),
        ]
        + [ANY] * len(deps),
        out_specs=pl.BlockSpec((1, rows, channels), lambda j: (j, 0, 0)),
        out_shape=jax.ShapeDtypeStruct((depth, rows, channels), BF16),
        compiler_params=BIG,
        cost_estimate=lasting(4),
    )(attended, weight, *deps)


def project_back(blocks, weight, deps=()):
    depth, rows, channels = blocks.shape

    def kernel(blocks_ref, weight_ref, *rest):
        out_ref, total = rest[-2:]
        j = pl.program_id(0)
        for start in range(0, rows, ROW_TILE):
            at = slice(start, start + ROW_TILE)
            term = dot_nt(blocks_ref[0, at], weight_ref[...])

            @pl.when(j == 0)
            def _():
                total[at] = term

            @pl.when((j > 0) & (j < depth - 1))
            def _():
                total[at] += term

            @pl.when(j == depth - 1)
            def _():
                out_ref[at] = (total[at] + term).astype(BF16)

    return pl.pallas_call(
        kernel,
        grid=(depth,),
        in_specs=[
            pl.BlockSpec((1, rows, channels), lambda j: (j, 0, 0)),
            pl.BlockSpec((channels, channels), lambda j: (0, j)),
        ]
        + [ANY] * len(deps),
        out_specs=pl.BlockSpec((rows, channels), lambda j: (0, 0)),
        out_shape=jax.ShapeDtypeStruct((rows, channels), BF16),
        scratch_shapes=[pltpu.VMEM((rows, channels), F32)],
        compiler_params=BIG,
        cost_estimate=lasting(6),
    )(blocks, weight, *deps)


def weight_terms(attended, blocks, count, deps=()):
    chunks = len(attended)
    depth, rows, channels = blocks[0].shape
    parts = count // depth
    columns = channels // parts

    def kernel(*refs):
        out_ref, turned = refs[-2:]

        @pl.when(pl.program_id(0) == 0)
        def _():
            for c in range(chunks):
                turned[c] = refs[c][...].T

        total = None
        for c in range(chunks):
            term = dot(turned[c], refs[chunks + c][0])
            total = term if total is None else total + term
        for p in range(parts):
            out_ref[0, p] = total[:, p * columns : (p + 1) * columns].astype(BF16)

    return pl.pallas_call(
        kernel,
        grid=(depth,),
        in_specs=[pl.BlockSpec((rows, channels), lambda j: (0, 0))] * chunks
        + [pl.BlockSpec((1, rows, channels), lambda j: (j, 0, 0))] * chunks
        + [ANY] * len(deps),
        out_specs=pl.BlockSpec((1, parts, channels, columns), lambda j: (j, 0, 0, 0)),
        out_shape=jax.ShapeDtypeStruct((depth, parts, channels, columns), BF16),
        scratch_shapes=[pltpu.VMEM((chunks, channels, rows), BF16)],
        compiler_params=BIG,
        cost_estimate=lasting(7),
    )(*attended, *blocks, *deps)


def core_sums(terms, near, core, deps=()):
    chips, _, channels, columns = terms.shape

    def kernel(core_ref, terms_ref, near_ref, *rest):
        rest[-1][...] = (terms_ref[:, 0].astype(F32) + near_ref[...].astype(F32)).astype(BF16)

    block = pl.BlockSpec((1, channels, columns), lambda i, core: (i, 0, 0))
    return pl.pallas_call(
        kernel,
        grid_spec=pltpu.PrefetchScalarGridSpec(
            num_scalar_prefetch=1,
            grid=(chips,),
            in_specs=[pl.BlockSpec((1, 1, channels, columns), lambda i, core: (i, core[0], 0, 0)), block]
            + [ANY] * len(deps),
            out_specs=block,
        ),
        out_shape=jax.ShapeDtypeStruct((chips, channels, columns), BF16),
        compiler_params=LIMIT,
        cost_estimate=lasting(2.6),
    )(core.reshape(1).astype(jnp.int32), terms, near, *deps)


def per_device(
    queries,
    keys,
    values,
    ref_keys,
    ref_values,
    rate_scale,
    rate_reach,
    window_start,
    out_weight,
    conv_taps,
    cotangent,
):
    frames, spatial, channels = queries.shape
    count, depth = lax.axis_size("frame"), lax.axis_size("head")
    place = lax.axis_index("frame")
    part = spatial // count // CHUNKS
    rows = count * frames * part
    reach = conv_taps.shape[0]
    line = (count * frames, part, channels)

    cot, own, blocks = [], [], []
    for c in range(CHUNKS):
        packed = to_positions([cotangent], c, count)
        cot.append(travel(packed if c == 0 else after(packed, own[-1])).reshape(line))
        own.append(mix_back(cot[c], conv_taps))
        blocks.append(lax.all_gather(own[c].reshape(rows, channels), "head", axis=0))

    even, odd = collect(after(jnp.stack([ref_keys, ref_values]), own[0]), count, [own[-1]])
    bias = temporal_bias(rate_scale, rate_reach, window_start)

    video, before = [], even
    for c in range(CHUNKS):
        packed = to_positions([queries, keys, values], c, count)
        video.append(travel(after(packed, before)))
        before = video[-1]

    last = []
    attended, saved, mixed = [], [], []

    def forward(c):
        nonlocal last
        out, *kept = attend(video[c], even, odd, bias, last)
        attended.append(out.reshape(rows, channels))
        saved.append(kept)
        shares = project(attended[c], out_weight)
        mixed.append(lax.psum_scatter(shares, "head", scatter_dimension=0, tiled=False))
        last = [shares]

    def pull(c):
        nonlocal last
        grad = project_back(blocks[c], out_weight, last)
        last = [grad]
        return grad.reshape(count, frames, part, channels)

    def backward(c, grad, arrays):
        nonlocal last
        results = attend_back(video[c], even, odd, saved[c], grad, arrays, last)
        last = [results[1]]
        return results

    forward(0)
    first_back, even_first, odd_first = backward(0, pull(0), 3)
    first_back = travel(first_back)
    forward(1)

    terms = weight_terms(attended, blocks, count, [*last, first_back])
    by_chip = terms.reshape(count // 2, 2, channels, terms.shape[3])
    core = place % 2
    near = swap(lax.dynamic_index_in_dim(by_chip, 1 - core, 1, keepdims=False), 1)
    sums = core_sums(by_chip, near, core)
    last = [sums]
    groups = [list(range(k, count, 2)) for k in range(2)]
    far = lax.all_to_all(sums, "frame", split_axis=0, concat_axis=0, axis_index_groups=groups, tiled=True)

    second_back, even_second, odd_second = backward(1, pull(1), 4)
    second_back, taps_first = mix(
        mixed[0].reshape(line), cot[0], conv_taps, count, room=second_back, deps=[*last, far]
    )
    second_back = travel(second_back)
    ref_grads = reduce_pieces(even_first + even_second, odd_first + odd_second, [second_back])
    final = mix(mixed[1].reshape(line), cot[1], conv_taps, count, taps_before=taps_first, deps=[ref_grads])
    final = travel(final)
    grad_weight = jnp.sum(far.astype(F32), axis=0)

    grads = [to_frames([first_back[:, a], second_back[:, a]]) for a in range(3)]
    held_rows = frames * part
    out = to_frames([second_back[:, 3], final[:, :held_rows].reshape(count, frames, part, channels)])
    taps_parts = jnp.sum(final[:, held_rows : held_rows + 2 * reach].astype(F32), axis=0)
    taps_sum = taps_parts[:reach] + taps_parts[reach:]
    return (out, *grads, ref_grads[0], ref_grads[1], grad_weight, taps_sum)


def solution(mesh):
    video = P("frame", None, "head")
    tokens = P("frame", "head")
    return jax.shard_map(
        per_device,
        mesh=mesh,
        in_specs=(
            video,
            video,
            video,
            tokens,
            tokens,
            P("head"),
            P("head"),
            P(),
            P("head", None),
            P(None, "head"),
            video,
        ),
        out_specs=(video, video, video, video, tokens, tokens, P("head", "frame"), P(None, "head")),
        check_vma=False,
    )
```
